32 devices in a mesh: seg: 8 (over z, x), sub: 4 (over y, core).
Axes of the slice: x: 2, y: 2, z: 4, core: 2. Of those that a mesh axis runs over, the one named last changes fastest.
Arguments:
- start_state: float32 [2, 27, 16384], P(None, None, ('seg', 'sub')), may hold values from -6 to 6
- right_side: float32 [2, 27, 16384], P(None, None, ('seg', 'sub')), may hold values from -3 to 3
- previous: float32 [27, 16384], P(None, ('seg', 'sub')), may hold values from -0.9 to 0.9
- refined: int32 [16384], P(('seg', 'sub')), may hold values 0 or 1
- old_cuts: int32 [8, 5], P('seg'), may hold values from 0 to 1024, as said below
- new_cuts: int32 [8, 5], P('seg'), may hold values from 0 to 1024, as said below
- face_links: int32 [6, 16384], P(None, ('seg', 'sub')), may hold values from -1 to 639
Outputs:
- smoothed: float32 [2, 27, 16384], P(None, None, ('seg', 'sub'))
The draws below stay inside these ranges and needn't reach their ends.
Inputs may be any that keep to these rules, and one draw needn't show every extreme that they name: `old_cuts`: each row begins with 0 and ends with 1024; consecutive cuts differ by 128 to 384, and in every row some difference is exactly 384. `new_cuts`: each row begins with 0 and ends with 1024 and never falls; every other cut lies within 64 positions of the old cut of the same index; in every row one cut lies exactly 64 before its old cut and the next one exactly 64 after, so that some device's new count is 512; no new count exceeds 512. `face_links`: entry (face, e) names the element across that face of new slot e: a value below 512 is a slot of the same device, 512 + g is slot g of device (s-1, u), 576 + g slot g of device (s+1, u), -1 the domain's boundary; faces in the order -x, +x, -y, +y, -z, +z. 1 marks a refined element.
All inputs are finite; a program needn't handle non-finite values. No bound on the sum of `refined` on one device may be relied on, other than what follows from the above.
Results may differ from the reference program's by a relative error of at most 0.0001.
Values sent between devices are 32-bit elements; how exact they have to be, the bound alone decides.
A program may use at most 64 MiB of HBM per device.

```python
import jax
import jax.numpy as jnp
import numpy as np
from jax import lax

NODES = 27
E_DEV = 256
SWEEPS = 3
CAP = 512
GHOST = 64
SLOTS = 16384
N_SEG = 8
N_SUB = 4


def cut_points(key):
    folded = jax.random.fold_in(key, 17)
    key_old, key_new, key_pick = jax.random.split(folded, 3)
    quarter = E_DEV // 4
    column = jnp.arange(N_SUB + 1, dtype=jnp.int32)[None, :]
    chosen = jax.random.randint(key_pick, (N_SEG, 1), 1, N_SUB - 1)
    interior = (column > 0) & (column < N_SUB)

    def jitter(sub_key):
        drawn = jax.random.randint(sub_key, (N_SEG, N_SUB + 1), -quarter, quarter + 1)
        drawn = jnp.where(column == chosen, -quarter, jnp.where(column == chosen + 1, quarter, drawn))
        return jnp.where(interior, drawn, 0)
    old_points = column * E_DEV + jitter(key_old)
    new_points = old_points + jitter(key_new)
    return (old_points.astype(jnp.int32), new_points.astype(jnp.int32))


def draw_old_cuts(key, part):
    return cut_points(key)[0]


def draw_new_cuts(key, part):
    return cut_points(key)[1]


def touch_ends(values, own_key, smallest, top_value):
    place = [jax.random.randint(jax.random.fold_in(own_key, axis), (), 0, length) for axis, length in enumerate(values.shape)]
    main_axis = values.shape.index(max(values.shape))
    neighbour = place[:main_axis] + [(place[main_axis] + 1) % values.shape[main_axis]] + place[main_axis + 1:]
    return values.at[tuple(place)].set(smallest).at[tuple(neighbour)].set(top_value)


def steps_of(rng, shape, cuts, low, high):
    gain, own = 1.0, jax.random.fold_in(rng, 6)
    for dim, shards_of in cuts:
        draws = jnp.exp(jax.random.uniform(jax.random.fold_in(own, dim), (shards_of,), jnp.float32, low / len(cuts), high / len(cuts)))
        gain = gain * jnp.repeat(draws, shape[dim] // shards_of).reshape([-1 if axis == dim else 1 for axis in range(len(shape))])
    return gain


def scatter_about(stream_key, extent, spread, most, cuts=(), held_as=jnp.bfloat16):
    values = jax.random.normal(stream_key, extent, jnp.float32) * spread
    if len(cuts) > 0:
        values = steps_of(stream_key, extent, cuts, -0.22, 0.18) * values
    return jnp.clip(values, min=-most, max=most).astype(held_as)


def setup_inputs(seed: int = 0) -> dict:
    keys = jax.random.split(jax.random.key(seed), 8)
    start_state = scatter_about(keys[0], (2, NODES, SLOTS), 1.0, 6.0, ((2, 32),), jnp.float32)
    right_side = scatter_about(keys[1], (2, NODES, SLOTS), 0.5, 3.0, ((2, 32),), jnp.float32)
    previous = jnp.clip(jax.random.uniform(keys[2], (NODES, SLOTS), jnp.float32, -0.9, 0.9) * steps_of(keys[2], (NODES, SLOTS), ((1, 32),), -0.4, 0.0), -0.9, 0.9)
    refined = touch_ends((jax.random.randint(keys[3], (SLOTS,), 0, 3) < 1).astype(jnp.int32), jax.random.fold_in(keys[3], 1), 0, 1)
    old_cuts = draw_old_cuts(jax.random.fold_in(keys[7], 71), 0)
    new_cuts = draw_new_cuts(jax.random.fold_in(keys[7], 71), 0)
    face_links = touch_ends(jax.random.randint(keys[6], (6, SLOTS), -1, CAP + 2 * GHOST), jax.random.fold_in(keys[6], 1), -1, (CAP + 2 * GHOST) - 1).astype(jnp.int32)
    return {"start_state": start_state, "right_side": right_side, "previous": previous, "refined": refined, "old_cuts": old_cuts, "new_cuts": new_cuts, "face_links": face_links}


time_step = 0.01
gradient_energy = 0.01
penalty = 2.0


def element_tables():
    weights = np.array([0.5, 2.0, 0.5])
    slope_table = np.array([[7.0, -8.0, 1.0], [-8.0, 16.0, -8.0], [1.0, -8.0, 7.0]]) / 6.0
    diagonal = np.array([[0.5, 0.0, 0.0], [0.0, 2.0, 0.0], [0.0, 0.0, 0.5]])
    stiffness = (np.kron(slope_table, np.kron(diagonal, diagonal)) + np.kron(diagonal, np.kron(slope_table, diagonal))
                 + np.kron(diagonal, np.kron(diagonal, slope_table)))
    mass_table = np.kron(weights, np.kron(weights, weights))
    across = np.zeros((6, 9), np.int32)
    face_map = np.zeros((27, 54))
    face_diag = np.zeros(27)
    for direction in range(3):
        for side_index in range(2):
            surface = 2 * direction + side_index
            for major_index in range(3):
                for minor_index in range(3):
                    inner_index = major_index * 3 + minor_index
                    near_side = [major_index, minor_index]
                    near_side.insert(direction, 2 * side_index)
                    far_side = [major_index, minor_index]
                    far_side.insert(direction, 2 - 2 * side_index)
                    near_node = near_side[0] * 9 + near_side[1] * 3 + near_side[2]
                    far_node = far_side[0] * 9 + far_side[1] * 3 + far_side[2]
                    across[surface, inner_index] = far_node
                    face_weight = weights[major_index] * weights[minor_index]
                    face_map[near_node, surface * 9 + inner_index] = face_weight
                    face_diag[near_node] += face_weight
    return (jnp.asarray(stiffness, jnp.float32), jnp.asarray(mass_table, jnp.float32),
            jnp.asarray(face_diag, jnp.float32), jnp.asarray(face_map, jnp.float32), across)


def laplace_part(iterate, face_links, tables, stiff_scale, ghost_width):
    stiffness, mass_table, face_diag, face_map, across = tables
    leading = iterate[..., :ghost_width]
    blank = jnp.zeros_like(leading[:, :, :1])
    below_rows = jnp.concatenate([blank, leading[:, :, :-1]], 2)
    above_rows = jnp.concatenate([leading[:, :, 1:], blank], 2)
    extended = jnp.concatenate([iterate, below_rows, above_rows], -1)
    pieces = []
    for surface in range(6):
        face_rows = extended[:, across[surface]]
        targets = face_links[surface]
        clamped = jnp.where(targets >= 0, targets, 0).astype(jnp.int32)
        wanted = jnp.broadcast_to(clamped[None, None], face_rows.shape[:2] + clamped.shape)
        picked = jnp.take_along_axis(face_rows, wanted, axis=-1)
        pieces.append(picked * (targets >= 0).astype(iterate.dtype))
    gathered = jnp.concatenate(pieces, 1)
    local_part = jnp.einsum("mn,fn...->fm...", stiffness, iterate, precision=lax.Precision.HIGHEST)
    coupled = jnp.einsum("mk,fk...->fm...", face_map, gathered, precision=lax.Precision.HIGHEST)
    return stiff_scale * (local_part + penalty * (face_diag[:, None, None, None] * iterate - coupled))


def reference(start_state, right_side, previous, refined, old_cuts, new_cuts, face_links):
    tables = element_tables()
    capacity = 2 * E_DEV
    ghost_width = E_DEV // 4
    packed = jnp.concatenate([start_state.reshape(54, -1), right_side.reshape(54, -1), previous,
                              refined.astype(jnp.float32)[None, :]], 0)
    slot_index = jnp.arange(capacity, dtype=jnp.int32)
    position = new_cuts[:, :N_SUB, None] + slot_index[None, None, :]
    new_counts = (new_cuts[:, 1:] - new_cuts[:, :N_SUB])[:, :, None]
    occupied = slot_index[None, None, :] < new_counts
    owner = jnp.sum((old_cuts[:, None, None, 1:N_SUB] <= position[..., None]).astype(jnp.int32), axis=-1, dtype=jnp.int32)
    owner_first = jnp.take_along_axis(old_cuts, owner.reshape(N_SEG, -1), axis=1).reshape(N_SEG, N_SUB, capacity)
    segment_index = jnp.arange(N_SEG, dtype=jnp.int32)[:, None, None]
    source_index = (segment_index * N_SUB + owner) * capacity + position - owner_first
    source_index = jnp.where(occupied, source_index, 0).astype(jnp.int32).reshape(-1)
    moved = jnp.take(packed, source_index, axis=1) * occupied.reshape(-1).astype(packed.dtype)[None, :]
    shape_five = (2, 27, N_SEG, N_SUB, capacity)
    iterate = moved[:54].reshape(shape_five)
    target = moved[54:108].reshape(shape_five)
    prior = moved[108:135].reshape(27, N_SEG, N_SUB, capacity)
    flag_row = moved[135].reshape(N_SEG, N_SUB, capacity)
    links = face_links.reshape(6, N_SEG, N_SUB, capacity)
    mass_scale = 1.0 - 0.875 * flag_row
    stiff_scale = 1.0 - 0.5 * flag_row
    mobility = 1.0 - prior * prior
    curvature = 3.0 * prior * prior - 1.0
    lumped = tables[1][:, None, None, None] * mass_scale[None]

    def operate(field):
        laplace = laplace_part(field, links, tables, stiff_scale, ghost_width)
        concentration = lumped * field[0] + time_step * mobility * laplace[1]
        potential = lumped * field[1] - curvature * (lumped * field[0]) - gradient_energy * laplace[0]
        return jnp.stack([concentration, potential], 0)

    center = 1.0
    half_width = 0.5
    spread_ratio = center / half_width
    weight_prev = 1.0 / spread_ratio
    update = jnp.zeros_like(iterate)
    for sweep_index in range(SWEEPS):
        residual = target - operate(iterate)
        scaled = residual / lumped[None]
        if sweep_index == 0:
            update = scaled / center
        else:
            weight_now = 1.0 / (2.0 * spread_ratio - weight_prev)
            update = (weight_now * weight_prev) * update + (2.0 * weight_now / half_width) * scaled
            weight_prev = weight_now
        iterate = iterate + update
    return iterate.reshape(2, 27, -1)
```

```python
import functools

import jax
import jax.numpy as jnp
import numpy as np
from jax import lax
from jax.experimental import pallas as pl
from jax.experimental.pallas import tpu as pltpu
from jax.sharding import PartitionSpec as P

SWEEPS = 3
MESH = pl.DeviceIdType.MESH
F32 = jnp.float32
BF16 = jnp.bfloat16
LANES = 128
HALF = 64
ROWS = 32
FACE_ROWS = 112

time_step = 0.01
gradient_energy = 0.01
penalty = 2.0


def element_tables():
    weights = np.array([0.5, 2.0, 0.5])
    slope_table = np.array([[7.0, -8.0, 1.0], [-8.0, 16.0, -8.0], [1.0, -8.0, 7.0]])
    diagonal = np.diag(weights)
    stiffness = (
        np.kron(slope_table, np.kron(diagonal, diagonal))
        + np.kron(diagonal, np.kron(slope_table, diagonal))
        + np.kron(diagonal, np.kron(diagonal, slope_table))
    )
    mass_table = np.kron(weights, np.kron(weights, weights))
    face_diag = np.zeros(27)
    select = np.zeros((FACE_ROWS, 2 * ROWS))
    scatter = np.zeros((2 * ROWS, FACE_ROWS))
    for direction in range(3):
        for side in range(2):
            surface = 2 * direction + side
            for major in range(3):
                for minor in range(3):
                    near = [major, minor]
                    near.insert(direction, 2 * side)
                    far = [major, minor]
                    far.insert(direction, 2 - 2 * side)
                    near_node = near[0] * 9 + near[1] * 3 + near[2]
                    far_node = far[0] * 9 + far[1] * 3 + far[2]
                    weight = weights[major] * weights[minor]
                    face_diag[near_node] += weight
                    for part in range(2):
                        row = surface * 18 + part * 9 + major * 3 + minor
                        select[row, part * ROWS + far_node] = -6.0 * penalty * weight
                        scatter[part * ROWS + near_node, row] = 1.0
    block = stiffness + 6.0 * penalty * np.diag(face_diag)
    local = np.zeros((2 * ROWS, 2 * ROWS))
    local[:27, :27] = block
    local[ROWS : ROWS + 27, ROWS : ROWS + 27] = block
    first = np.concatenate([local, select], 0)
    first = np.concatenate([first, first], 1)
    second = np.concatenate([scatter, scatter], 1)
    inverse = np.zeros((ROWS, LANES))
    inverse[:27] = 1.0 / mass_table[:, None]
    return first, second, inverse


def split(values):
    high = values.astype(BF16)
    low = (values - high.astype(F32)).astype(BF16)
    return jnp.concatenate([high, low], 0)


def kernel(
    n_seg, n_sub, old_cuts, new_cuts, start, right, prev, refined, links, first, second, inverse,
    out, fields, flags, link_buf, first_buf, second_buf, inverse_buf,
    index_buf, block_buf, head_out, tail_out, head_in, tail_in, ghost_out, ghost_in,
    moved_buf, face_buf, load_sem, head_sem, tail_sem, ghost_send, ghost_recv,
):
    seg, sub = lax.axis_index("seg"), lax.axis_index("sub")
    capacity = links.shape[1]
    blocks = capacity // LANES

    loads = [
        pltpu.make_async_copy(source, target, load_sem.at[i])
        for i, (source, target) in enumerate(
            [
                (start, fields.at[pl.ds(0, 2)]),
                (right, fields.at[pl.ds(2, 2)]),
                (prev, fields.at[4]),
                (refined, flags),
                (links, link_buf),
                (first, first_buf),
                (second, second_buf),
                (inverse, inverse_buf),
            ]
        )
    ]
    for load in loads:
        load.start()

    head_in[...] = jnp.zeros_like(head_in)
    tail_in[...] = jnp.zeros_like(tail_in)
    ghost_in[...] = jnp.zeros_like(ghost_in)

    left = (sub > 0, (seg, sub - 1))
    after = (sub < n_sub - 1, (seg, sub + 1))
    below = (seg > 0, (seg - 1, sub))
    above = (seg < n_seg - 1, (seg + 1, sub))
    sides = (left, after, below, above)
    barrier = pltpu.get_barrier_semaphore()
    for there, place in sides:
        @pl.when(there)
        def _(place=place):
            pl.semaphore_signal(barrier, inc=1, device_id=place, device_id_type=MESH)

    head_copy = pltpu.make_async_remote_copy(
        src_ref=head_out, dst_ref=head_in, send_sem=head_sem.at[0], recv_sem=head_sem.at[1],
        device_id=left[1], device_id_type=MESH)
    tail_copy = pltpu.make_async_remote_copy(
        src_ref=tail_out, dst_ref=tail_in, send_sem=tail_sem.at[0], recv_sem=tail_sem.at[1],
        device_id=after[1], device_id_type=MESH)
    up_copies, down_copies = [], []
    for sweep in range(SWEEPS):
        up_copies.append(pltpu.make_async_remote_copy(
            src_ref=ghost_out.at[sweep], dst_ref=ghost_in.at[sweep, 0],
            send_sem=ghost_send.at[sweep, 0], recv_sem=ghost_recv.at[sweep, 0],
            device_id=above[1], device_id_type=MESH))
        down_copies.append(pltpu.make_async_remote_copy(
            src_ref=ghost_out.at[sweep], dst_ref=ghost_in.at[sweep, 1],
            send_sem=ghost_send.at[sweep, 1], recv_sem=ghost_recv.at[sweep, 1],
            device_id=below[1], device_id_type=MESH))

    old_first, old_end = old_cuts[0, sub], old_cuts[0, sub + 1]
    new_first, new_end = new_cuts[0, sub], new_cuts[0, sub + 1]
    left_first = old_cuts[0, jnp.maximum(sub - 1, 0)]
    old_count, new_count = old_end - old_first, new_end - new_first
    shift = new_first - old_first
    mask = LANES - 1
    lane = lax.broadcasted_iota(jnp.int32, (8, LANES), 1)
    row = lax.broadcasted_iota(jnp.int32, (8, LANES), 0)

    def wide(values, rows):
        return jnp.broadcast_to(values[:1], (rows, LANES))

    def lanes(rows):
        return lax.broadcasted_iota(jnp.int32, (rows, LANES), 1)

    for i in range(4):
        loads[i].wait()

    pad = jnp.zeros((ROWS - 27, LANES), F32)
    row32 = lax.broadcasted_iota(jnp.int32, (ROWS, LANES), 0)

    def packed(b):
        cols = pl.ds(b * LANES, LANES)
        parts = [jnp.concatenate([fields[g, :, cols], pad], 0) for g in range(5)]
        flag = flags[:, cols].astype(F32)
        parts[4] = jnp.where(row32 == 27, jnp.broadcast_to(flag, (ROWS, LANES)), parts[4])
        return jnp.concatenate(parts, 0)

    all_rows = 5 * ROWS
    upper = all_rows // 2
    whole = [packed(b) for b in range(blocks)]
    lane_u = lanes(upper)
    head_out[...] = jnp.where(lane_u < HALF, whole[0][:upper], pltpu.roll(whole[0][upper:], HALF, 1))
    tail = whole[0]
    lane_a = lanes(all_rows)
    window = (lane_u >= old_count - HALF) & (lane_u < old_count)
    for b in range(1, blocks):
        slot = lane_a + b * LANES
        inside = (slot >= old_count - HALF) & (slot < old_count)
        tail = jnp.where(inside, whole[b], tail)
        slot_u = lane_u + b * LANES
        window = window | ((slot_u >= old_count - HALF) & (slot_u < old_count))
    tail_out[...] = jnp.where(window, tail[:upper], pltpu.roll(tail[upper:], HALF, 1))

    pl.semaphore_wait(
        barrier,
        (jnp.minimum(sub, 1) + jnp.minimum(n_sub - 1 - sub, 1)
         + jnp.minimum(seg, 1) + jnp.minimum(n_seg - 1 - seg, 1)),
    )

    @pl.when(after[0])
    def _():
        tail_copy.start()

    @pl.when(left[0])
    def _():
        head_copy.start()

    turn = (-shift) & mask
    turned = [pltpu.roll(w, turn, 1) for w in whole]
    came_from = lane_a + shift
    for b in range(blocks):
        mine = turned[b]
        if b > 0:
            mine = jnp.where(came_from < 0, turned[b - 1], mine)
        if b < blocks - 1:
            mine = jnp.where(came_from >= LANES, turned[b + 1], mine)
        moved_buf[:, b * LANES : (b + 1) * LANES] = mine

    loads[4].wait()
    for b in range(blocks):
        cols = pl.ds(b * LANES, LANES)
        rows = [jnp.broadcast_to(link_buf[f : f + 1, cols], (8, LANES)) for f in range(6)]
        parts = []
        for k in range(FACE_ROWS // 8):
            f0, f1 = min(8 * k // 18, 5), min((8 * k + 7) // 18, 5)
            part = rows[f0]
            if f1 != f0:
                part = jnp.where(row < f1 * 18 - 8 * k, part, rows[f1])
            parts.append(part)
        link = jnp.concatenate(parts, 0)
        index_buf[:, cols] = link & mask
        block_buf[:, cols] = link >> 7
    for i in range(5, 8):
        loads[i].wait()

    @pl.when(left[0])
    def _():
        tail_copy.wait_recv()

    offset = left_first - new_first
    from_left = jnp.concatenate(
        [
            pltpu.roll(tail_in[...], offset & mask, 1),
            pltpu.roll(tail_in[...], (offset + HALF) & mask, 1),
        ],
        0,
    )
    block0 = jnp.where(lane_a < -shift, from_left, moved_buf[:, :LANES])
    block0 = jnp.where(lane_a < new_count, block0, 0.0)

    def send(sweep, c, mu):
        lane32 = lanes(ROWS)
        ghost_out[sweep] = jnp.where(lane32 < HALF, c, pltpu.roll(mu, HALF, 1))

        @pl.when(above[0])
        def _():
            up_copies[sweep].start()

        @pl.when(below[0])
        def _():
            down_copies[sweep].start()

    send(0, block0[:ROWS], block0[ROWS : 2 * ROWS])
    moved_buf[:, :LANES] = block0

    @pl.when(after[0])
    def _():
        head_copy.wait_recv()

    edge = old_end - new_first
    from_right = jnp.concatenate(
        [
            pltpu.roll(head_in[...], edge & mask, 1),
            pltpu.roll(head_in[...], (edge + HALF) & mask, 1),
        ],
        0,
    )
    state, coefficients = [], []
    inverse_mass = inverse_buf[...]
    for b in range(blocks):
        slot = lane_a + b * LANES
        whole_b = moved_buf[:, b * LANES : (b + 1) * LANES]
        whole_b = jnp.where(slot >= edge, from_right, whole_b)
        whole_b = jnp.where(slot < new_count, whole_b, 0.0)
        state.append(whole_b[: 2 * ROWS])
        prior = whole_b[4 * ROWS :]
        flag = jnp.broadcast_to(prior[27:28], (ROWS, LANES))
        inverse_lumped = inverse_mass * (1.0 + 7.0 * flag)
        stiff = (1.0 - 0.5 * flag) * inverse_lumped * (1.0 / 6.0)
        coefficients.append(
            (
                whole_b[2 * ROWS : 3 * ROWS] * inverse_lumped,
                whole_b[3 * ROWS : 4 * ROWS] * inverse_lumped,
                time_step * stiff * (1.0 - prior * prior),
                gradient_energy * stiff,
                3.0 * prior * prior - 1.0,
            )
        )

    spread_ratio = 2.0
    half_width = 0.5
    weight_prev = 1.0 / spread_ratio
    update = [None] * blocks
    first_table, second_table = first_buf[...], second_buf[...]
    lane32 = lanes(ROWS)
    for sweep in range(SWEEPS):
        last = sweep == SWEEPS - 1
        product = jnp.dot(
            first_table, jnp.concatenate([split(v) for v in state], 1), preferred_element_type=F32
        )
        near = product[: 2 * ROWS]
        sources = [product[2 * ROWS :, b * LANES : (b + 1) * LANES] for b in range(blocks)]

        def pick(total, source, number, b):
            cols = slice(b * LANES, (b + 1) * LANES)
            index = index_buf[:, cols]
            got = jnp.take_along_axis(source, index, axis=1, mode="promise_in_bounds")
            return jnp.where(block_buf[:, cols] == number, got, total)

        faces = []
        for b in range(blocks):
            total = jnp.zeros((FACE_ROWS, LANES), F32)
            for number in range(blocks):
                total = pick(total, sources[number], number, b)
            faces.append(total)

        @pl.when(below[0])
        def _():
            up_copies[sweep].wait_recv()

        @pl.when(above[0])
        def _():
            down_copies[sweep].wait_recv()

        got_below, got_above = ghost_in[sweep, 0], ghost_in[sweep, 1]
        ghost = jnp.concatenate(
            [
                jnp.where(lane32 < HALF, got_below, pltpu.roll(got_above, HALF, 1)),
                jnp.where(lane32 < HALF, pltpu.roll(got_below, HALF, 1), got_above),
            ],
            0,
        )
        ghost_faces = jnp.dot(first_table[2 * ROWS :], split(ghost), preferred_element_type=F32)

        weight_now = 1.0 / (2.0 * spread_ratio - weight_prev)
        for b in range(blocks):
            total = pick(faces[b], ghost_faces, blocks, b)
            coupled = jnp.dot(second_table, split(total), preferred_element_type=F32)
            laplace = near[:, b * LANES : (b + 1) * LANES] + coupled
            side_c, side_mu, mobile, stiff, curvature = coefficients[b]
            c, mu = state[b][:ROWS], state[b][ROWS:]
            scaled = jnp.concatenate(
                [
                    side_c - c - mobile * laplace[ROWS:],
                    side_mu - mu + curvature * c + stiff * laplace[:ROWS],
                ],
                0,
            )
            if sweep == 0:
                update[b] = scaled
            else:
                update[b] = (
                    weight_now * weight_prev * update[b] + (2.0 * weight_now / half_width) * scaled
                )
            state[b] = state[b] + update[b]
            if last:
                cols = pl.ds(b * LANES, LANES)
                out[0, :, cols] = state[b][:27]
                out[1, :, cols] = state[b][ROWS : ROWS + 27]
            elif b == 0:
                send(sweep + 1, state[0][:ROWS], state[0][ROWS:])
        if sweep > 0:
            weight_prev = weight_now

    @pl.when(left[0])
    def _():
        head_copy.wait_send()

    @pl.when(after[0])
    def _():
        tail_copy.wait_send()

    for sweep in range(SWEEPS):
        @pl.when(above[0])
        def _():
            up_copies[sweep].wait_send()

        @pl.when(below[0])
        def _():
            down_copies[sweep].wait_send()


def local(n_seg, n_sub, start_state, right_side, previous, refined, old_cuts, new_cuts, face_links):
    capacity = start_state.shape[-1]
    first, second, inverse = element_tables()
    any_space = pl.BlockSpec(memory_space=pl.ANY)
    smem = pl.BlockSpec(memory_space=pltpu.SMEM)
    packed_rows = 5 * ROWS // 2
    return pl.pallas_call(
        functools.partial(kernel, n_seg, n_sub),
        out_shape=jax.ShapeDtypeStruct((2, 27, capacity), F32),
        in_specs=[smem, smem] + [any_space] * 8,
        out_specs=pl.BlockSpec(memory_space=pltpu.VMEM),
        scratch_shapes=[
            pltpu.VMEM((5, 27, capacity), F32),
            pltpu.VMEM((1, capacity), jnp.int32),
            pltpu.VMEM((6, capacity), jnp.int32),
            pltpu.VMEM(first.shape, BF16),
            pltpu.VMEM(second.shape, BF16),
            pltpu.VMEM(inverse.shape, F32),
            pltpu.VMEM((FACE_ROWS, capacity), jnp.int32),
            pltpu.VMEM((FACE_ROWS, capacity), jnp.int32),
            pltpu.VMEM((packed_rows, LANES), F32),
            pltpu.VMEM((packed_rows, LANES), F32),
            pltpu.VMEM((packed_rows, LANES), F32),
            pltpu.VMEM((packed_rows, LANES), F32),
            pltpu.VMEM((SWEEPS, ROWS, LANES), F32),
            pltpu.VMEM((SWEEPS, 2, ROWS, LANES), F32),
            pltpu.VMEM((5 * ROWS, capacity), F32),
            pltpu.VMEM((8, LANES), F32),
            pltpu.SemaphoreType.DMA((8,)),
            pltpu.SemaphoreType.DMA((2,)),
            pltpu.SemaphoreType.DMA((2,)),
            pltpu.SemaphoreType.DMA((SWEEPS, 2)),
            pltpu.SemaphoreType.DMA((SWEEPS, 2)),
        ],
        compiler_params=pltpu.CompilerParams(
            collective_id=0, has_side_effects=True, vmem_limit_bytes=16 * 1024 * 1024
        ),
        name="smooth",
    )(
        old_cuts, new_cuts, start_state, right_side, previous, refined.reshape(1, capacity),
        face_links, jnp.asarray(first, BF16), jnp.asarray(second, BF16), jnp.asarray(inverse, F32),
    )


def solution(mesh):
    placed = (
        P(None, None, ("seg", "sub")),
        P(None, None, ("seg", "sub")),
        P(None, ("seg", "sub")),
        P(("seg", "sub")),
        P("seg", None),
        P("seg", None),
        P(None, ("seg", "sub")),
    )
    return jax.shard_map(
        functools.partial(local, mesh.shape["seg"], mesh.shape["sub"]),
        mesh=mesh, in_specs=placed, out_specs=P(None, None, ("seg", "sub")), check_vma=False,
    )
```

```python
import functools

import jax
import jax.numpy as jnp
import numpy as np
from jax import lax
from jax.experimental import pallas as pl
from jax.experimental.pallas import tpu as pltpu
from jax.sharding import PartitionSpec as P

SWEEPS = 3
MESH = pl.DeviceIdType.MESH
F32 = jnp.float32
BF16 = jnp.bfloat16
LANES = 128
HALF = 64
ROWS = 32
FACE_ROWS = 112

time_step = 0.01
gradient_energy = 0.01
penalty = 2.0


def element_tables():
    weights = np.array([0.5, 2.0, 0.5])
    slope_table = np.array([[7.0, -8.0, 1.0], [-8.0, 16.0, -8.0], [1.0, -8.0, 7.0]])
    diagonal = np.diag(weights)
    stiffness = (
        np.kron(slope_table, np.kron(diagonal, diagonal))
        + np.kron(diagonal, np.kron(slope_table, diagonal))
        + np.kron(diagonal, np.kron(diagonal, slope_table))
    )
    mass_table = np.kron(weights, np.kron(weights, weights))
    face_diag = np.zeros(27)
    select = np.zeros((FACE_ROWS, 2 * ROWS))
    scatter = np.zeros((2 * ROWS, FACE_ROWS))
    for direction in range(3):
        for side in range(2):
            surface = 2 * direction + side
            for major in range(3):
                for minor in range(3):
                    near = [major, minor]
                    near.insert(direction, 2 * side)
                    far = [major, minor]
                    far.insert(direction, 2 - 2 * side)
                    near_node = near[0] * 9 + near[1] * 3 + near[2]
                    far_node = far[0] * 9 + far[1] * 3 + far[2]
                    weight = weights[major] * weights[minor]
                    face_diag[near_node] += weight
                    for part in range(2):
                        row = surface * 18 + part * 9 + major * 3 + minor
                        select[row, part * ROWS + far_node] = -6.0 * penalty * weight
                        scatter[part * ROWS + near_node, row] = 1.0
    block = stiffness + 6.0 * penalty * np.diag(face_diag)
    local = np.zeros((2 * ROWS, 2 * ROWS))
    local[:27, :27] = block
    local[ROWS : ROWS + 27, ROWS : ROWS + 27] = block
    first = np.concatenate([local, select], 0)
    first = np.concatenate([first, first], 1)
    second = np.concatenate([scatter, scatter], 1)
    inverse = np.zeros((ROWS, LANES))
    inverse[:27] = 1.0 / mass_table[:, None]
    return first, second, inverse


def split(values):
    high = values.astype(BF16)
    low = (values - high.astype(F32)).astype(BF16)
    return jnp.concatenate([high, low], 0)


def kernel(
    n_seg, n_sub, old_cuts, new_cuts, start, right, prev, refined, links, first, second, inverse,
    out, state_buf, side_buf, prior_buf, flags, link_buf, first_buf, second_buf, inverse_buf,
    index_buf, block_buf, head_out, tail_out, head_in, tail_in, ghost_out, ghost_in,
    moved_buf, face_buf, load_sem, head_sem, tail_sem, ghost_send, ghost_recv,
):
    seg, sub = lax.axis_index("seg"), lax.axis_index("sub")
    capacity = links.shape[1]
    blocks = capacity // LANES

    loads = [
        pltpu.make_async_copy(source, target, load_sem.at[i])
        for i, (source, target) in enumerate(
            [
                (start, state_buf),
                (right, side_buf),
                (prev, prior_buf),
                (refined, flags),
                (links, link_buf),
                (first, first_buf),
                (second, second_buf),
                (inverse, inverse_buf),
            ]
        )
    ]
    for load in loads:
        load.start()

    head_in[...] = jnp.zeros_like(head_in)
    tail_in[...] = jnp.zeros_like(tail_in)
    ghost_in[...] = jnp.zeros_like(ghost_in)

    left = (sub > 0, (seg, sub - 1))
    after = (sub < n_sub - 1, (seg, sub + 1))
    below = (seg > 0, (seg - 1, sub))
    above = (seg < n_seg - 1, (seg + 1, sub))
    sides = (left, after, below, above)
    barrier = pltpu.get_barrier_semaphore()
    for there, place in sides:
        @pl.when(there)
        def _(place=place):
            pl.semaphore_signal(barrier, inc=1, device_id=place, device_id_type=MESH)

    head_copy = pltpu.make_async_remote_copy(
        src_ref=head_out, dst_ref=head_in, send_sem=head_sem.at[0], recv_sem=head_sem.at[1],
        device_id=left[1], device_id_type=MESH)
    tail_copy = pltpu.make_async_remote_copy(
        src_ref=tail_out, dst_ref=tail_in, send_sem=tail_sem.at[0], recv_sem=tail_sem.at[1],
        device_id=after[1], device_id_type=MESH)
    up_copies, down_copies = [], []
    for sweep in range(SWEEPS):
        up_copies.append(pltpu.make_async_remote_copy(
            src_ref=ghost_out.at[sweep], dst_ref=ghost_in.at[sweep, 0],
            send_sem=ghost_send.at[sweep, 0], recv_sem=ghost_recv.at[sweep, 0],
            device_id=above[1], device_id_type=MESH))
        down_copies.append(pltpu.make_async_remote_copy(
            src_ref=ghost_out.at[sweep], dst_ref=ghost_in.at[sweep, 1],
            send_sem=ghost_send.at[sweep, 1], recv_sem=ghost_recv.at[sweep, 1],
            device_id=below[1], device_id_type=MESH))

    old_first, old_end = old_cuts[0, sub], old_cuts[0, sub + 1]
    new_first, new_end = new_cuts[0, sub], new_cuts[0, sub + 1]
    left_first = old_cuts[0, jnp.maximum(sub - 1, 0)]
    old_count, new_count = old_end - old_first, new_end - new_first
    shift = new_first - old_first
    mask = LANES - 1
    lane = lax.broadcasted_iota(jnp.int32, (8, LANES), 1)
    row = lax.broadcasted_iota(jnp.int32, (8, LANES), 0)

    def wide(values, rows):
        return jnp.broadcast_to(values[:1], (rows, LANES))

    def lanes(rows):
        return lax.broadcasted_iota(jnp.int32, (rows, LANES), 1)

    for i in range(4):
        loads[i].wait()

    pad = jnp.zeros((ROWS - 27, LANES), F32)
    row32 = lax.broadcasted_iota(jnp.int32, (ROWS, LANES), 0)

    def packed(b):
        cols = pl.ds(b * LANES, LANES)
        parts = [
            jnp.concatenate([rows, pad], 0)
            for rows in (
                state_buf[pl.ds(2 * b, 27, stride=2 * blocks), :],
                state_buf[pl.ds(2 * b + 1, 27, stride=2 * blocks), :],
                side_buf[pl.ds(2 * b, 27, stride=2 * blocks), :],
                side_buf[pl.ds(2 * b + 1, 27, stride=2 * blocks), :],
                prior_buf[:, cols],
            )
        ]
        flag = flags[:, cols].astype(F32)
        parts[4] = jnp.where(row32 == 27, jnp.broadcast_to(flag, (ROWS, LANES)), parts[4])
        return jnp.concatenate(parts, 0)

    all_rows = 5 * ROWS
    upper = all_rows // 2
    whole = [packed(b) for b in range(blocks)]
    lane_u = lanes(upper)
    head_out[...] = jnp.where(lane_u < HALF, whole[0][:upper], pltpu.roll(whole[0][upper:], HALF, 1))
    tail = whole[0]
    lane_a = lanes(all_rows)
    window = (lane_u >= old_count - HALF) & (lane_u < old_count)
    for b in range(1, blocks):
        slot = lane_a + b * LANES
        inside = (slot >= old_count - HALF) & (slot < old_count)
        tail = jnp.where(inside, whole[b], tail)
        slot_u = lane_u + b * LANES
        window = window | ((slot_u >= old_count - HALF) & (slot_u < old_count))
    tail_out[...] = jnp.where(window, tail[:upper], pltpu.roll(tail[upper:], HALF, 1))

    pl.semaphore_wait(
        barrier,
        (jnp.minimum(sub, 1) + jnp.minimum(n_sub - 1 - sub, 1)
         + jnp.minimum(seg, 1) + jnp.minimum(n_seg - 1 - seg, 1)),
    )

    @pl.when(after[0])
    def _():
        tail_copy.start()

    @pl.when(left[0])
    def _():
        head_copy.start()

    turn = (-shift) & mask
    turned = [pltpu.roll(w, turn, 1) for w in whole]
    came_from = lane_a + shift
    for b in range(blocks):
        mine = turned[b]
        if b > 0:
            mine = jnp.where(came_from < 0, turned[b - 1], mine)
        if b < blocks - 1:
            mine = jnp.where(came_from >= LANES, turned[b + 1], mine)
        moved_buf[:, b * LANES : (b + 1) * LANES] = mine

    loads[4].wait()
    for b in range(blocks):
        cols = pl.ds(b * LANES, LANES)
        rows = [jnp.broadcast_to(link_buf[f : f + 1, cols], (8, LANES)) for f in range(6)]
        parts = []
        for k in range(FACE_ROWS // 8):
            f0, f1 = min(8 * k // 18, 5), min((8 * k + 7) // 18, 5)
            part = rows[f0]
            if f1 != f0:
                part = jnp.where(row < f1 * 18 - 8 * k, part, rows[f1])
            parts.append(part)
        link = jnp.concatenate(parts, 0)
        index_buf[:, cols] = link & mask
        block_buf[:, cols] = link >> 7
    for i in range(5, 8):
        loads[i].wait()

    @pl.when(left[0])
    def _():
        tail_copy.wait_recv()

    offset = left_first - new_first
    from_left = jnp.concatenate(
        [
            pltpu.roll(tail_in[...], offset & mask, 1),
            pltpu.roll(tail_in[...], (offset + HALF) & mask, 1),
        ],
        0,
    )
    block0 = jnp.where(lane_a < -shift, from_left, moved_buf[:, :LANES])
    block0 = jnp.where(lane_a < new_count, block0, 0.0)

    def send(sweep, c, mu):
        lane32 = lanes(ROWS)
        ghost_out[sweep] = jnp.where(lane32 < HALF, c, pltpu.roll(mu, HALF, 1))

        @pl.when(above[0])
        def _():
            up_copies[sweep].start()

        @pl.when(below[0])
        def _():
            down_copies[sweep].start()

    send(0, block0[:ROWS], block0[ROWS : 2 * ROWS])
    moved_buf[:, :LANES] = block0

    @pl.when(after[0])
    def _():
        head_copy.wait_recv()

    edge = old_end - new_first
    from_right = jnp.concatenate(
        [
            pltpu.roll(head_in[...], edge & mask, 1),
            pltpu.roll(head_in[...], (edge + HALF) & mask, 1),
        ],
        0,
    )
    state, coefficients = [], []
    inverse_mass = inverse_buf[...]
    for b in range(blocks):
        slot = lane_a + b * LANES
        whole_b = moved_buf[:, b * LANES : (b + 1) * LANES]
        whole_b = jnp.where(slot >= edge, from_right, whole_b)
        whole_b = jnp.where(slot < new_count, whole_b, 0.0)
        state.append(whole_b[: 2 * ROWS])
        prior = whole_b[4 * ROWS :]
        flag = jnp.broadcast_to(prior[27:28], (ROWS, LANES))
        inverse_lumped = inverse_mass * (1.0 + 7.0 * flag)
        stiff = (1.0 - 0.5 * flag) * inverse_lumped * (1.0 / 6.0)
        coefficients.append(
            (
                whole_b[2 * ROWS : 3 * ROWS] * inverse_lumped,
                whole_b[3 * ROWS : 4 * ROWS] * inverse_lumped,
                time_step * stiff * (1.0 - prior * prior),
                gradient_energy * stiff,
                3.0 * prior * prior - 1.0,
            )
        )

    spread_ratio = 2.0
    half_width = 0.5
    weight_prev = 1.0 / spread_ratio
    update = [None] * blocks
    first_table, second_table = first_buf[...], second_buf[...]
    lane32 = lanes(ROWS)
    for sweep in range(SWEEPS):
        last = sweep == SWEEPS - 1
        product = jnp.dot(
            first_table, jnp.concatenate([split(v) for v in state], 1), preferred_element_type=F32
        )
        near = product[: 2 * ROWS]
        sources = [product[2 * ROWS :, b * LANES : (b + 1) * LANES] for b in range(blocks)]

        def pick(total, source, number, b):
            cols = slice(b * LANES, (b + 1) * LANES)
            index = index_buf[:, cols]
            got = jnp.take_along_axis(source, index, axis=1, mode="promise_in_bounds")
            return jnp.where(block_buf[:, cols] == number, got, total)

        faces = []
        for b in range(blocks):
            total = jnp.zeros((FACE_ROWS, LANES), F32)
            for number in range(blocks):
                total = pick(total, sources[number], number, b)
            faces.append(total)

        @pl.when(below[0])
        def _():
            up_copies[sweep].wait_recv()

        @pl.when(above[0])
        def _():
            down_copies[sweep].wait_recv()

        got_below, got_above = ghost_in[sweep, 0], ghost_in[sweep, 1]
        ghost = jnp.concatenate(
            [
                jnp.where(lane32 < HALF, got_below, pltpu.roll(got_above, HALF, 1)),
                jnp.where(lane32 < HALF, pltpu.roll(got_below, HALF, 1), got_above),
            ],
            0,
        )
        ghost_faces = jnp.dot(first_table[2 * ROWS :], split(ghost), preferred_element_type=F32)

        weight_now = 1.0 / (2.0 * spread_ratio - weight_prev)
        for b in range(blocks):
            total = pick(faces[b], ghost_faces, blocks, b)
            coupled = jnp.dot(second_table, split(total), preferred_element_type=F32)
            laplace = near[:, b * LANES : (b + 1) * LANES] + coupled
            side_c, side_mu, mobile, stiff, curvature = coefficients[b]
            c, mu = state[b][:ROWS], state[b][ROWS:]
            scaled = jnp.concatenate(
                [
                    side_c - c - mobile * laplace[ROWS:],
                    side_mu - mu + curvature * c + stiff * laplace[:ROWS],
                ],
                0,
            )
            if sweep == 0:
                update[b] = scaled
            else:
                update[b] = (
                    weight_now * weight_prev * update[b] + (2.0 * weight_now / half_width) * scaled
                )
            state[b] = state[b] + update[b]
            if last:
                out[pl.ds(2 * b, 27, stride=2 * blocks), :] = state[b][:27]
                out[pl.ds(2 * b + 1, 27, stride=2 * blocks), :] = state[b][ROWS : ROWS + 27]
            elif b == 0:
                send(sweep + 1, state[0][:ROWS], state[0][ROWS:])
        if sweep > 0:
            weight_prev = weight_now

    @pl.when(left[0])
    def _():
        head_copy.wait_send()

    @pl.when(after[0])
    def _():
        tail_copy.wait_send()

    for sweep in range(SWEEPS):
        @pl.when(above[0])
        def _():
            up_copies[sweep].wait_send()

        @pl.when(below[0])
        def _():
            down_copies[sweep].wait_send()


def local(n_seg, n_sub, start_state, right_side, previous, refined, old_cuts, new_cuts, face_links):
    capacity = start_state.shape[-1]
    first, second, inverse = element_tables()
    any_space = pl.BlockSpec(memory_space=pl.ANY)
    smem = pl.BlockSpec(memory_space=pltpu.SMEM)
    packed_rows = 5 * ROWS // 2
    blocks = capacity // LANES

    def by_node(array):
        array = array.transpose(1, 0, 2).reshape(27, 2, blocks, LANES)
        return array.transpose(0, 2, 1, 3).reshape(54 * blocks, LANES)

    smoothed = pl.pallas_call(
        functools.partial(kernel, n_seg, n_sub),
        out_shape=pltpu.VMEM((54 * blocks, LANES), F32),
        in_specs=[smem, smem] + [any_space] * 8,
        out_specs=pl.BlockSpec(memory_space=pltpu.VMEM),
        scratch_shapes=[
            pltpu.VMEM((54 * blocks, LANES), F32),
            pltpu.VMEM((54 * blocks, LANES), F32),
            pltpu.VMEM((27, capacity), F32),
            pltpu.VMEM((1, capacity), jnp.int32),
            pltpu.VMEM((6, capacity), jnp.int32),
            pltpu.VMEM(first.shape, BF16),
            pltpu.VMEM(second.shape, BF16),
            pltpu.VMEM(inverse.shape, F32),
            pltpu.VMEM((FACE_ROWS, capacity), jnp.int32),
            pltpu.VMEM((FACE_ROWS, capacity), jnp.int32),
            pltpu.VMEM((packed_rows, LANES), F32),
            pltpu.VMEM((packed_rows, LANES), F32),
            pltpu.VMEM((packed_rows, LANES), F32),
            pltpu.VMEM((packed_rows, LANES), F32),
            pltpu.VMEM((SWEEPS, ROWS, LANES), F32),
            pltpu.VMEM((SWEEPS, 2, ROWS, LANES), F32),
            pltpu.VMEM((5 * ROWS, capacity), F32),
            pltpu.VMEM((8, LANES), F32),
            pltpu.SemaphoreType.DMA((8,)),
            pltpu.SemaphoreType.DMA((2,)),
            pltpu.SemaphoreType.DMA((2,)),
            pltpu.SemaphoreType.DMA((SWEEPS, 2)),
            pltpu.SemaphoreType.DMA((SWEEPS, 2)),
        ],
        compiler_params=pltpu.CompilerParams(
            collective_id=0, has_side_effects=True, vmem_limit_bytes=60 * 1024 * 1024
        ),
        name="smooth",
    )(
        old_cuts, new_cuts, by_node(start_state), by_node(right_side), previous,
        refined.reshape(1, capacity),
        face_links, jnp.asarray(first, BF16), jnp.asarray(second, BF16), jnp.asarray(inverse, F32),
    )
    smoothed = smoothed.reshape(27, blocks, 2, LANES).transpose(2, 0, 1, 3)
    return smoothed.reshape(2, 27, capacity)


def solution(mesh):
    placed = (
        P(None, None, ("seg", "sub")),
        P(None, None, ("seg", "sub")),
        P(None, ("seg", "sub")),
        P(("seg", "sub")),
        P("seg", None),
        P("seg", None),
        P(None, ("seg", "sub")),
    )
    return jax.shard_map(
        functools.partial(local, mesh.shape["seg"], mesh.shape["sub"]),
        mesh=mesh, in_specs=placed, out_specs=P(None, None, ("seg", "sub")), check_vma=False,
    )
```

```python
import functools

import jax
import jax.numpy as jnp
import numpy as np
from jax import lax
from jax.experimental import pallas as pl
from jax.experimental.pallas import tpu as pltpu
from jax.sharding import PartitionSpec as P

SWEEPS = 3
MESH = pl.DeviceIdType.MESH
F32 = jnp.float32
BF16 = jnp.bfloat16
LANES = 128
HALF = 64
ROWS = 32
FACE_ROWS = 112

time_step = 0.01
gradient_energy = 0.01
penalty = 2.0


def element_tables():
    weights = np.array([0.5, 2.0, 0.5])
    slope_table = np.array([[7.0, -8.0, 1.0], [-8.0, 16.0, -8.0], [1.0, -8.0, 7.0]])
    diagonal = np.diag(weights)
    stiffness = (
        np.kron(slope_table, np.kron(diagonal, diagonal))
        + np.kron(diagonal, np.kron(slope_table, diagonal))
        + np.kron(diagonal, np.kron(diagonal, slope_table))
    )
    mass_table = np.kron(weights, np.kron(weights, weights))
    face_diag = np.zeros(27)
    select = np.zeros((FACE_ROWS, 2 * ROWS))
    scatter = np.zeros((2 * ROWS, FACE_ROWS))
    for direction in range(3):
        for side in range(2):
            surface = 2 * direction + side
            for major in range(3):
                for minor in range(3):
                    near = [major, minor]
                    near.insert(direction, 2 * side)
                    far = [major, minor]
                    far.insert(direction, 2 - 2 * side)
                    near_node = near[0] * 9 + near[1] * 3 + near[2]
                    far_node = far[0] * 9 + far[1] * 3 + far[2]
                    weight = weights[major] * weights[minor]
                    face_diag[near_node] += weight
                    for part in range(2):
                        row = surface * 18 + part * 9 + major * 3 + minor
                        select[row, part * ROWS + far_node] = -6.0 * penalty * weight
                        scatter[part * ROWS + near_node, row] = 1.0
    block = stiffness + 6.0 * penalty * np.diag(face_diag)
    local = np.zeros((2 * ROWS, 2 * ROWS))
    local[:27, :27] = block
    local[ROWS : ROWS + 27, ROWS : ROWS + 27] = block
    first = np.concatenate([local, select], 0)
    first = np.concatenate([first, first], 1)
    second = np.concatenate([scatter, scatter], 1)
    inverse = np.zeros((ROWS, LANES))
    inverse[:27] = 1.0 / mass_table[:, None]
    return first, second, inverse


def split(values):
    high = values.astype(BF16)
    low = (values - high.astype(F32)).astype(BF16)
    return jnp.concatenate([high, low], 0)


def kernel(
    n_seg, n_sub, old_cuts, new_cuts, start, right, prev, refined, links, first, second, inverse,
    out, state_buf, side_buf, prior_buf, flags, link_buf, first_buf, second_buf, inverse_buf,
    index_buf, block_buf, head_out, tail_out, head_in, tail_in, ghost_out, ghost_in,
    corner_out, corner_in, moved_buf, load_sem, head_sem, tail_sem, ghost_send, ghost_recv,
    corner_send, corner_recv,
):
    seg, sub = lax.axis_index("seg"), lax.axis_index("sub")
    capacity = links.shape[1]
    blocks = capacity // LANES

    loads = [
        pltpu.make_async_copy(source, target, load_sem.at[i])
        for i, (source, target) in enumerate(
            [
                (start, state_buf),
                (right, side_buf),
                (prev, prior_buf),
                (refined, flags),
                (links, link_buf),
                (first, first_buf),
                (second, second_buf),
                (inverse, inverse_buf),
            ]
        )
    ]
    for load in loads:
        load.start()

    head_in[...] = jnp.zeros_like(head_in)
    tail_in[...] = jnp.zeros_like(tail_in)
    ghost_in[...] = jnp.zeros_like(ghost_in)
    corner_in[...] = jnp.zeros_like(corner_in)

    left = (sub > 0, (seg, sub - 1))
    after = (sub < n_sub - 1, (seg, sub + 1))
    below = (seg > 0, (seg - 1, sub))
    above = (seg < n_seg - 1, (seg + 1, sub))
    above_after = (above[0] & after[0], (seg + 1, sub + 1))
    below_after = (below[0] & after[0], (seg - 1, sub + 1))
    above_left = (above[0] & left[0], (seg + 1, sub - 1))
    below_left = (below[0] & left[0], (seg - 1, sub - 1))
    sides = (left, after, below, above, above_left, below_left)
    barrier = pltpu.get_barrier_semaphore()
    for there, place in sides:
        @pl.when(there)
        def _(place=place):
            pl.semaphore_signal(barrier, inc=1, device_id=place, device_id_type=MESH)

    head_copy = pltpu.make_async_remote_copy(
        src_ref=head_out, dst_ref=head_in, send_sem=head_sem.at[0], recv_sem=head_sem.at[1],
        device_id=left[1], device_id_type=MESH)
    tail_copy = pltpu.make_async_remote_copy(
        src_ref=tail_out, dst_ref=tail_in, send_sem=tail_sem.at[0], recv_sem=tail_sem.at[1],
        device_id=after[1], device_id_type=MESH)
    up_copies, down_copies = [], []
    for sweep in range(SWEEPS):
        up_copies.append(pltpu.make_async_remote_copy(
            src_ref=ghost_out.at[sweep], dst_ref=ghost_in.at[sweep, 0],
            send_sem=ghost_send.at[sweep, 0], recv_sem=ghost_recv.at[sweep, 0],
            device_id=above[1], device_id_type=MESH))
        down_copies.append(pltpu.make_async_remote_copy(
            src_ref=ghost_out.at[sweep], dst_ref=ghost_in.at[sweep, 1],
            send_sem=ghost_send.at[sweep, 1], recv_sem=ghost_recv.at[sweep, 1],
            device_id=below[1], device_id_type=MESH))

    corner_up = pltpu.make_async_remote_copy(
        src_ref=corner_out, dst_ref=corner_in.at[0], send_sem=corner_send.at[0],
        recv_sem=corner_recv.at[0], device_id=above_after[1], device_id_type=MESH)
    corner_down = pltpu.make_async_remote_copy(
        src_ref=corner_out, dst_ref=corner_in.at[1], send_sem=corner_send.at[1],
        recv_sem=corner_recv.at[1], device_id=below_after[1], device_id_type=MESH)

    old_first, old_end = old_cuts[0, sub], old_cuts[0, sub + 1]
    new_first, new_end = new_cuts[0, sub], new_cuts[0, sub + 1]
    left_first = old_cuts[0, jnp.maximum(sub - 1, 0)]
    old_count, new_count = old_end - old_first, new_end - new_first
    shift = new_first - old_first
    mask = LANES - 1
    lane = lax.broadcasted_iota(jnp.int32, (8, LANES), 1)
    row = lax.broadcasted_iota(jnp.int32, (8, LANES), 0)

    def wide(values, rows):
        return jnp.broadcast_to(values[:1], (rows, LANES))

    def lanes(rows):
        return lax.broadcasted_iota(jnp.int32, (rows, LANES), 1)

    for i in range(4):
        loads[i].wait()

    pad = jnp.zeros((ROWS - 27, LANES), F32)
    row32 = lax.broadcasted_iota(jnp.int32, (ROWS, LANES), 0)

    def packed(b):
        cols = pl.ds(b * LANES, LANES)
        parts = [
            jnp.concatenate([rows, pad], 0)
            for rows in (
                state_buf[pl.ds(2 * b, 27, stride=2 * blocks), :],
                state_buf[pl.ds(2 * b + 1, 27, stride=2 * blocks), :],
                side_buf[pl.ds(2 * b, 27, stride=2 * blocks), :],
                side_buf[pl.ds(2 * b + 1, 27, stride=2 * blocks), :],
                prior_buf[:, cols],
            )
        ]
        flag = flags[:, cols].astype(F32)
        parts[4] = jnp.where(row32 == 27, jnp.broadcast_to(flag, (ROWS, LANES)), parts[4])
        return jnp.concatenate(parts, 0)

    all_rows = 5 * ROWS
    upper = all_rows // 2
    whole = [packed(b) for b in range(blocks)]
    lane_u = lanes(upper)
    head_out[...] = jnp.where(lane_u < HALF, whole[0][:upper], pltpu.roll(whole[0][upper:], HALF, 1))
    tail = whole[0]
    lane_a = lanes(all_rows)
    window = (lane_u >= old_count - HALF) & (lane_u < old_count)
    for b in range(1, blocks):
        slot = lane_a + b * LANES
        inside = (slot >= old_count - HALF) & (slot < old_count)
        tail = jnp.where(inside, whole[b], tail)
        slot_u = lane_u + b * LANES
        window = window | ((slot_u >= old_count - HALF) & (slot_u < old_count))
    tail_out[...] = jnp.where(window, tail[:upper], pltpu.roll(tail[upper:], HALF, 1))

    turn = (-shift) & mask
    lane32 = lanes(ROWS)
    slot32 = lane32 & (HALF - 1)

    def both(rows, amount):
        return jnp.where(
            lane32 < HALF,
            pltpu.roll(rows[:ROWS], amount & mask, 1),
            pltpu.roll(rows[ROWS : 2 * ROWS], (amount + HALF) & mask, 1),
        )

    ghost_out[0] = jnp.where(
        (slot32 >= -shift) & (slot32 < new_count), both(whole[0], turn), 0.0
    )
    next_count = new_cuts[0, jnp.minimum(sub + 2, n_sub)] - new_end
    corner_out[...] = jnp.where(
        (slot32 < old_end - new_end) & (slot32 < next_count), both(tail, old_first - new_end), 0.0
    )

    seg_sides = jnp.minimum(seg, 1) + jnp.minimum(n_seg - 1 - seg, 1)
    has_after = jnp.minimum(n_sub - 1 - sub, 1)
    pl.semaphore_wait(barrier, jnp.minimum(sub, 1) + has_after + seg_sides * (1 + has_after))

    @pl.when(after[0])
    def _():
        tail_copy.start()

    @pl.when(left[0])
    def _():
        head_copy.start()

    for there, copy in (
        (above_after[0], corner_up), (below_after[0], corner_down),
        (above[0], up_copies[0]), (below[0], down_copies[0]),
    ):
        @pl.when(there)
        def _(copy=copy):
            copy.start()

    turned = [pltpu.roll(w, turn, 1) for w in whole]
    came_from = lane_a + shift
    for b in range(blocks):
        mine = turned[b]
        if b > 0:
            mine = jnp.where(came_from < 0, turned[b - 1], mine)
        if b < blocks - 1:
            mine = jnp.where(came_from >= LANES, turned[b + 1], mine)
        moved_buf[:, b * LANES : (b + 1) * LANES] = mine

    loads[4].wait()
    for b in range(blocks):
        cols = pl.ds(b * LANES, LANES)
        rows = [jnp.broadcast_to(link_buf[f : f + 1, cols], (8, LANES)) for f in range(6)]
        parts = []
        for k in range(FACE_ROWS // 8):
            f0, f1 = min(8 * k // 18, 5), min((8 * k + 7) // 18, 5)
            part = rows[f0]
            if f1 != f0:
                part = jnp.where(row < f1 * 18 - 8 * k, part, rows[f1])
            parts.append(part)
        link = jnp.concatenate(parts, 0)
        index_buf[:, cols] = link & mask
        block_buf[:, cols] = link >> 7
    for i in range(5, 8):
        loads[i].wait()

    @pl.when(left[0])
    def _():
        tail_copy.wait_recv()

    offset = left_first - new_first
    from_left = jnp.concatenate(
        [
            pltpu.roll(tail_in[...], offset & mask, 1),
            pltpu.roll(tail_in[...], (offset + HALF) & mask, 1),
        ],
        0,
    )
    block0 = jnp.where(lane_a < -shift, from_left, moved_buf[:, :LANES])

    def send(sweep, c, mu):
        ghost_out[sweep] = jnp.where(lane32 < HALF, c, pltpu.roll(mu, HALF, 1))

        @pl.when(above[0])
        def _():
            up_copies[sweep].start()

        @pl.when(below[0])
        def _():
            down_copies[sweep].start()

    moved_buf[:, :LANES] = block0

    @pl.when(after[0])
    def _():
        head_copy.wait_recv()

    edge = old_end - new_first
    from_right = jnp.concatenate(
        [
            pltpu.roll(head_in[...], edge & mask, 1),
            pltpu.roll(head_in[...], (edge + HALF) & mask, 1),
        ],
        0,
    )
    state, coefficients = [], []
    inverse_mass = inverse_buf[...]
    for b in range(blocks):
        slot = lane_a + b * LANES
        whole_b = moved_buf[:, b * LANES : (b + 1) * LANES]
        whole_b = jnp.where(slot >= edge, from_right, whole_b)
        whole_b = jnp.where(slot < new_count, whole_b, 0.0)
        state.append(whole_b[: 2 * ROWS])
        prior = whole_b[4 * ROWS :]
        flag = jnp.broadcast_to(prior[27:28], (ROWS, LANES))
        inverse_lumped = inverse_mass * (1.0 + 7.0 * flag)
        stiff = (1.0 - 0.5 * flag) * inverse_lumped * (1.0 / 6.0)
        coefficients.append(
            (
                whole_b[2 * ROWS : 3 * ROWS] * inverse_lumped,
                whole_b[3 * ROWS : 4 * ROWS] * inverse_lumped,
                time_step * stiff * (1.0 - prior * prior),
                gradient_energy * stiff,
                3.0 * prior * prior - 1.0,
            )
        )

    spread_ratio = 2.0
    half_width = 0.5
    weight_prev = 1.0 / spread_ratio
    update = [None] * blocks
    first_table, second_table = first_buf[...], second_buf[...]
    for sweep in range(SWEEPS):
        last = sweep == SWEEPS - 1
        product = jnp.dot(
            first_table, jnp.concatenate([split(v) for v in state], 1), preferred_element_type=F32
        )
        near = product[: 2 * ROWS]
        sources = [product[2 * ROWS :, b * LANES : (b + 1) * LANES] for b in range(blocks)]

        def pick(total, source, number, b):
            cols = slice(b * LANES, (b + 1) * LANES)
            index = index_buf[:, cols]
            got = jnp.take_along_axis(source, index, axis=1, mode="promise_in_bounds")
            return jnp.where(block_buf[:, cols] == number, got, total)

        faces = []
        for b in range(blocks):
            total = jnp.zeros((FACE_ROWS, LANES), F32)
            for number in range(blocks):
                total = pick(total, sources[number], number, b)
            faces.append(total)

        @pl.when(below[0])
        def _():
            up_copies[sweep].wait_recv()

        @pl.when(above[0])
        def _():
            down_copies[sweep].wait_recv()

        got_below, got_above = ghost_in[sweep, 0], ghost_in[sweep, 1]
        if sweep == 0:
            @pl.when(below_left[0])
            def _():
                corner_up.wait_recv()

            @pl.when(above_left[0])
            def _():
                corner_down.wait_recv()

            got_below = got_below + corner_in[0]
            got_above = got_above + corner_in[1]
        ghost = jnp.concatenate(
            [
                jnp.where(lane32 < HALF, got_below, pltpu.roll(got_above, HALF, 1)),
                jnp.where(lane32 < HALF, pltpu.roll(got_below, HALF, 1), got_above),
            ],
            0,
        )
        ghost_faces = jnp.dot(first_table[2 * ROWS :], split(ghost), preferred_element_type=F32)

        weight_now = 1.0 / (2.0 * spread_ratio - weight_prev)
        for b in range(blocks):
            total = pick(faces[b], ghost_faces, blocks, b)
            coupled = jnp.dot(second_table, split(total), preferred_element_type=F32)
            laplace = near[:, b * LANES : (b + 1) * LANES] + coupled
            side_c, side_mu, mobile, stiff, curvature = coefficients[b]
            c, mu = state[b][:ROWS], state[b][ROWS:]
            scaled = jnp.concatenate(
                [
                    side_c - c - mobile * laplace[ROWS:],
                    side_mu - mu + curvature * c + stiff * laplace[:ROWS],
                ],
                0,
            )
            if sweep == 0:
                update[b] = scaled
            else:
                update[b] = (
                    weight_now * weight_prev * update[b] + (2.0 * weight_now / half_width) * scaled
                )
            state[b] = state[b] + update[b]
            if last:
                out[pl.ds(2 * b, 27, stride=2 * blocks), :] = state[b][:27]
                out[pl.ds(2 * b + 1, 27, stride=2 * blocks), :] = state[b][ROWS : ROWS + 27]
            elif b == 0:
                send(sweep + 1, state[0][:ROWS], state[0][ROWS:])
        if sweep > 0:
            weight_prev = weight_now

    @pl.when(left[0])
    def _():
        head_copy.wait_send()

    @pl.when(after[0])
    def _():
        tail_copy.wait_send()

    @pl.when(above_after[0])
    def _():
        corner_up.wait_send()

    @pl.when(below_after[0])
    def _():
        corner_down.wait_send()

    for sweep in range(SWEEPS):
        @pl.when(above[0])
        def _():
            up_copies[sweep].wait_send()

        @pl.when(below[0])
        def _():
            down_copies[sweep].wait_send()


def local(n_seg, n_sub, start_state, right_side, previous, refined, old_cuts, new_cuts, face_links):
    capacity = start_state.shape[-1]
    first, second, inverse = element_tables()
    any_space = pl.BlockSpec(memory_space=pl.ANY)
    smem = pl.BlockSpec(memory_space=pltpu.SMEM)
    packed_rows = 5 * ROWS // 2
    blocks = capacity // LANES

    def by_node(array):
        array = array.transpose(1, 0, 2).reshape(27, 2, blocks, LANES)
        return array.transpose(0, 2, 1, 3).reshape(54 * blocks, LANES)

    smoothed = pl.pallas_call(
        functools.partial(kernel, n_seg, n_sub),
        out_shape=pltpu.VMEM((54 * blocks, LANES), F32),
        in_specs=[smem, smem] + [any_space] * 8,
        out_specs=pl.BlockSpec(memory_space=pltpu.VMEM),
        scratch_shapes=[
            pltpu.VMEM((54 * blocks, LANES), F32),
            pltpu.VMEM((54 * blocks, LANES), F32),
            pltpu.VMEM((27, capacity), F32),
            pltpu.VMEM((1, capacity), jnp.int32),
            pltpu.VMEM((6, capacity), jnp.int32),
            pltpu.VMEM(first.shape, BF16),
            pltpu.VMEM(second.shape, BF16),
            pltpu.VMEM(inverse.shape, F32),
            pltpu.VMEM((FACE_ROWS, capacity), jnp.int32),
            pltpu.VMEM((FACE_ROWS, capacity), jnp.int32),
            pltpu.VMEM((packed_rows, LANES), F32),
            pltpu.VMEM((packed_rows, LANES), F32),
            pltpu.VMEM((packed_rows, LANES), F32),
            pltpu.VMEM((packed_rows, LANES), F32),
            pltpu.VMEM((SWEEPS, ROWS, LANES), F32),
            pltpu.VMEM((SWEEPS, 2, ROWS, LANES), F32),
            pltpu.VMEM((ROWS, LANES), F32),
            pltpu.VMEM((2, ROWS, LANES), F32),
            pltpu.VMEM((5 * ROWS, capacity), F32),
            pltpu.SemaphoreType.DMA((8,)),
            pltpu.SemaphoreType.DMA((2,)),
            pltpu.SemaphoreType.DMA((2,)),
            pltpu.SemaphoreType.DMA((SWEEPS, 2)),
            pltpu.SemaphoreType.DMA((SWEEPS, 2)),
            pltpu.SemaphoreType.DMA((2,)),
            pltpu.SemaphoreType.DMA((2,)),
        ],
        compiler_params=pltpu.CompilerParams(
            collective_id=0, has_side_effects=True, vmem_limit_bytes=60 * 1024 * 1024
        ),
        name="smooth",
    )(
        old_cuts, new_cuts, by_node(start_state), by_node(right_side), previous,
        refined.reshape(1, capacity),
        face_links, jnp.asarray(first, BF16), jnp.asarray(second, BF16), jnp.asarray(inverse, F32),
    )
    smoothed = smoothed.reshape(27, blocks, 2, LANES).transpose(2, 0, 1, 3)
    return smoothed.reshape(2, 27, capacity)


def solution(mesh):
    placed = (
        P(None, None, ("seg", "sub")),
        P(None, None, ("seg", "sub")),
        P(None, ("seg", "sub")),
        P(("seg", "sub")),
        P("seg", None),
        P("seg", None),
        P(None, ("seg", "sub")),
    )
    return jax.shard_map(
        functools.partial(local, mesh.shape["seg"], mesh.shape["sub"]),
        mesh=mesh, in_specs=placed, out_specs=P(None, None, ("seg", "sub")), check_vma=False,
    )
```

```python
import functools

import jax
import jax.numpy as jnp
import numpy as np
from jax import lax
from jax.experimental import pallas as pl
from jax.experimental.pallas import tpu as pltpu
from jax.sharding import PartitionSpec as P

SWEEPS = 3
MESH = pl.DeviceIdType.MESH
F32 = jnp.float32
BF16 = jnp.bfloat16
LANES = 128
HALF = 64
ROWS = 32
FACE_ROWS = 112

time_step = 0.01
gradient_energy = 0.01
penalty = 2.0


def element_tables():
    weights = np.array([0.5, 2.0, 0.5])
    slope_table = np.array([[7.0, -8.0, 1.0], [-8.0, 16.0, -8.0], [1.0, -8.0, 7.0]])
    diagonal = np.diag(weights)
    stiffness = (
        np.kron(slope_table, np.kron(diagonal, diagonal))
        + np.kron(diagonal, np.kron(slope_table, diagonal))
        + np.kron(diagonal, np.kron(diagonal, slope_table))
    )
    mass_table = np.kron(weights, np.kron(weights, weights))
    face_diag = np.zeros(27)
    select = np.zeros((FACE_ROWS, 2 * ROWS))
    scatter = np.zeros((2 * ROWS, FACE_ROWS))
    for direction in range(3):
        for side in range(2):
            surface = 2 * direction + side
            for major in range(3):
                for minor in range(3):
                    near = [major, minor]
                    near.insert(direction, 2 * side)
                    far = [major, minor]
                    far.insert(direction, 2 - 2 * side)
                    near_node = near[0] * 9 + near[1] * 3 + near[2]
                    far_node = far[0] * 9 + far[1] * 3 + far[2]
                    weight = weights[major] * weights[minor]
                    face_diag[near_node] += weight
                    for part in range(2):
                        row = surface * 18 + part * 9 + major * 3 + minor
                        select[row, part * ROWS + far_node] = -6.0 * penalty * weight
                        scatter[part * ROWS + near_node, row] = 1.0
    block = stiffness + 6.0 * penalty * np.diag(face_diag)
    local = np.zeros((2 * ROWS, 2 * ROWS))
    local[:27, :27] = block
    local[ROWS : ROWS + 27, ROWS : ROWS + 27] = block
    first = np.concatenate([local, select], 0)
    first = np.concatenate([first, first], 1)
    second = np.concatenate([scatter, scatter], 1)
    inverse = np.zeros((ROWS, LANES))
    inverse[:27] = 1.0 / mass_table[:, None]
    return first, second, inverse


def split(values):
    high = values.astype(BF16)
    low = (values - high.astype(F32)).astype(BF16)
    return jnp.concatenate([high, low], 0)


def kernel(
    n_seg, n_sub, old_cuts, new_cuts, start, right, prev, refined, links, first, second, inverse,
    out, state_buf, side_buf, prior_buf, flags, link_buf, first_buf, second_buf, inverse_buf,
    index_buf, block_buf, head_out0, tail_out0, head_in0, tail_in0,
    head_out1, tail_out1, head_in1, tail_in1, ghost_out, ghost_in,
    corner_out, corner_in, moved_buf, load_sem, head_sem, tail_sem, ghost_send, ghost_recv,
    corner_send, corner_recv,
):
    seg, sub = lax.axis_index("seg"), lax.axis_index("sub")
    capacity = links.shape[1]
    blocks = capacity // LANES

    loads = [
        pltpu.make_async_copy(source, target, load_sem.at[i])
        for i, (source, target) in enumerate(
            [
                (start, state_buf),
                (right, side_buf),
                (prev, prior_buf),
                (refined, flags),
                (links, link_buf),
                (first, first_buf),
                (second, second_buf),
                (inverse, inverse_buf),
            ]
        )
    ]
    for load in loads:
        load.start()

    for arriving in (head_in0, tail_in0, head_in1, tail_in1):
        arriving[...] = jnp.zeros_like(arriving)
    ghost_in[...] = jnp.zeros_like(ghost_in)
    corner_in[...] = jnp.zeros_like(corner_in)

    left = (sub > 0, (seg, sub - 1))
    after = (sub < n_sub - 1, (seg, sub + 1))
    below = (seg > 0, (seg - 1, sub))
    above = (seg < n_seg - 1, (seg + 1, sub))
    above_after = (above[0] & after[0], (seg + 1, sub + 1))
    below_after = (below[0] & after[0], (seg - 1, sub + 1))
    above_left = (above[0] & left[0], (seg + 1, sub - 1))
    below_left = (below[0] & left[0], (seg - 1, sub - 1))
    sides = (left, after, below, above, above_left, below_left)
    barrier = pltpu.get_barrier_semaphore()
    for there, place in sides:
        @pl.when(there)
        def _(place=place):
            pl.semaphore_signal(barrier, inc=1, device_id=place, device_id_type=MESH)

    head_copies = [
        pltpu.make_async_remote_copy(
            src_ref=source, dst_ref=target, send_sem=head_sem.at[i, 0], recv_sem=head_sem.at[i, 1],
            device_id=left[1], device_id_type=MESH)
        for i, (source, target) in enumerate([(head_out0, head_in0), (head_out1, head_in1)])
    ]
    tail_copies = [
        pltpu.make_async_remote_copy(
            src_ref=source, dst_ref=target, send_sem=tail_sem.at[i, 0], recv_sem=tail_sem.at[i, 1],
            device_id=after[1], device_id_type=MESH)
        for i, (source, target) in enumerate([(tail_out0, tail_in0), (tail_out1, tail_in1)])
    ]
    up_copies, down_copies = [], []
    for sweep in range(SWEEPS):
        up_copies.append(pltpu.make_async_remote_copy(
            src_ref=ghost_out.at[sweep], dst_ref=ghost_in.at[sweep, 0],
            send_sem=ghost_send.at[sweep, 0], recv_sem=ghost_recv.at[sweep, 0],
            device_id=above[1], device_id_type=MESH))
        down_copies.append(pltpu.make_async_remote_copy(
            src_ref=ghost_out.at[sweep], dst_ref=ghost_in.at[sweep, 1],
            send_sem=ghost_send.at[sweep, 1], recv_sem=ghost_recv.at[sweep, 1],
            device_id=below[1], device_id_type=MESH))

    corner_up = pltpu.make_async_remote_copy(
        src_ref=corner_out, dst_ref=corner_in.at[0], send_sem=corner_send.at[0],
        recv_sem=corner_recv.at[0], device_id=above_after[1], device_id_type=MESH)
    corner_down = pltpu.make_async_remote_copy(
        src_ref=corner_out, dst_ref=corner_in.at[1], send_sem=corner_send.at[1],
        recv_sem=corner_recv.at[1], device_id=below_after[1], device_id_type=MESH)

    old_first, old_end = old_cuts[0, sub], old_cuts[0, sub + 1]
    new_first, new_end = new_cuts[0, sub], new_cuts[0, sub + 1]
    left_first = old_cuts[0, jnp.maximum(sub - 1, 0)]
    old_count, new_count = old_end - old_first, new_end - new_first
    shift = new_first - old_first
    mask = LANES - 1
    lane = lax.broadcasted_iota(jnp.int32, (8, LANES), 1)
    row = lax.broadcasted_iota(jnp.int32, (8, LANES), 0)

    def wide(values, rows):
        return jnp.broadcast_to(values[:1], (rows, LANES))

    def lanes(rows):
        return lax.broadcasted_iota(jnp.int32, (rows, LANES), 1)

    pad = jnp.zeros((ROWS - 27, LANES), F32)
    row32 = lax.broadcasted_iota(jnp.int32, (ROWS, LANES), 0)

    def component(buffer, b, part):
        rows = buffer[pl.ds(2 * b + part, 27, stride=2 * blocks), :]
        return jnp.concatenate([rows, pad], 0)

    def pack_edges(whole, head_out, tail_out):
        count = whole[0].shape[0]
        upper = count // 2
        lane_u, lane_a = lanes(upper), lanes(count)
        head_out[...] = jnp.where(
            lane_u < HALF, whole[0][:upper], pltpu.roll(whole[0][upper:], HALF, 1)
        )
        tail = whole[0]
        window = (lane_u >= old_count - HALF) & (lane_u < old_count)
        for b in range(1, blocks):
            slot = lane_a + b * LANES
            inside = (slot >= old_count - HALF) & (slot < old_count)
            tail = jnp.where(inside, whole[b], tail)
            slot_u = lane_u + b * LANES
            window = window | ((slot_u >= old_count - HALF) & (slot_u < old_count))
        tail_out[...] = jnp.where(window, tail[:upper], pltpu.roll(tail[upper:], HALF, 1))
        return tail

    def start_edges(i):
        @pl.when(after[0])
        def _():
            tail_copies[i].start()

        @pl.when(left[0])
        def _():
            head_copies[i].start()

    def rotate(whole, first_row):
        turned = [pltpu.roll(w, turn, 1) for w in whole]
        came_from = lanes(whole[0].shape[0]) + shift
        for b in range(blocks):
            mine = turned[b]
            if b > 0:
                mine = jnp.where(came_from < 0, turned[b - 1], mine)
            if b < blocks - 1:
                mine = jnp.where(came_from >= LANES, turned[b + 1], mine)
            rows = slice(first_row, first_row + whole[0].shape[0])
            moved_buf[rows, b * LANES : (b + 1) * LANES] = mine

    def from_edge(arrived, amount):
        return jnp.concatenate(
            [
                pltpu.roll(arrived[...], amount & mask, 1),
                pltpu.roll(arrived[...], (amount + HALF) & mask, 1),
            ],
            0,
        )

    edge = old_end - new_first

    def arrive(i, first_row, count, head_in, tail_in):
        @pl.when(left[0])
        def _():
            tail_copies[i].wait_recv()

        @pl.when(after[0])
        def _():
            head_copies[i].wait_recv()

        from_left = from_edge(tail_in, left_first - new_first)
        from_right = from_edge(head_in, edge)
        lane_a = lanes(count)
        result = []
        for b in range(blocks):
            slot = lane_a + b * LANES
            part = moved_buf[first_row : first_row + count, b * LANES : (b + 1) * LANES]
            if b == 0:
                part = jnp.where(slot < -shift, from_left, part)
            part = jnp.where(slot >= edge, from_right, part)
            result.append(jnp.where(slot < new_count, part, 0.0))
        return result

    loads[0].wait()
    whole = [
        jnp.concatenate([component(state_buf, b, 0), component(state_buf, b, 1)], 0)
        for b in range(blocks)
    ]
    tail = pack_edges(whole, head_out0, tail_out0)

    turn = (-shift) & mask
    lane32 = lanes(ROWS)
    slot32 = lane32 & (HALF - 1)

    def both(rows, amount):
        return jnp.where(
            lane32 < HALF,
            pltpu.roll(rows[:ROWS], amount & mask, 1),
            pltpu.roll(rows[ROWS : 2 * ROWS], (amount + HALF) & mask, 1),
        )

    ghost_out[0] = jnp.where(
        (slot32 >= -shift) & (slot32 < new_count), both(whole[0], turn), 0.0
    )
    next_count = new_cuts[0, jnp.minimum(sub + 2, n_sub)] - new_end
    corner_out[...] = jnp.where(
        (slot32 < old_end - new_end) & (slot32 < next_count), both(tail, old_first - new_end), 0.0
    )

    seg_sides = jnp.minimum(seg, 1) + jnp.minimum(n_seg - 1 - seg, 1)
    has_after = jnp.minimum(n_sub - 1 - sub, 1)
    pl.semaphore_wait(barrier, jnp.minimum(sub, 1) + has_after + seg_sides * (1 + has_after))

    start_edges(0)

    for there, copy in (
        (above_after[0], corner_up), (below_after[0], corner_down),
        (above[0], up_copies[0]), (below[0], down_copies[0]),
    ):
        @pl.when(there)
        def _(copy=copy):
            copy.start()

    for i in range(1, 4):
        loads[i].wait()
    others = []
    for b in range(blocks):
        cols = pl.ds(b * LANES, LANES)
        flag = flags[:, cols].astype(F32)
        prior = jnp.concatenate([prior_buf[:, cols], pad], 0)
        prior = jnp.where(row32 == 27, jnp.broadcast_to(flag, (ROWS, LANES)), prior)
        others.append(
            jnp.concatenate([component(side_buf, b, 0), component(side_buf, b, 1), prior], 0)
        )
    pack_edges(others, head_out1, tail_out1)
    start_edges(1)
    rotate(whole, 0)

    loads[4].wait()
    for b in range(blocks):
        cols = pl.ds(b * LANES, LANES)
        rows = [jnp.broadcast_to(link_buf[f : f + 1, cols], (8, LANES)) for f in range(6)]
        parts = []
        for k in range(FACE_ROWS // 8):
            f0, f1 = min(8 * k // 18, 5), min((8 * k + 7) // 18, 5)
            part = rows[f0]
            if f1 != f0:
                part = jnp.where(row < f1 * 18 - 8 * k, part, rows[f1])
            parts.append(part)
        link = jnp.concatenate(parts, 0)
        index_buf[:, cols] = link & mask
        block_buf[:, cols] = link >> 7
    for i in range(5, 8):
        loads[i].wait()

    def send(sweep, c, mu):
        ghost_out[sweep] = jnp.where(lane32 < HALF, c, pltpu.roll(mu, HALF, 1))

        @pl.when(above[0])
        def _():
            up_copies[sweep].start()

        @pl.when(below[0])
        def _():
            down_copies[sweep].start()

    state = arrive(0, 0, 2 * ROWS, head_in0, tail_in0)
    rotate(others, 2 * ROWS)

    def coefficients_of():
        result = []
        inverse_mass = inverse_buf[...]
        for part in arrive(1, 2 * ROWS, 3 * ROWS, head_in1, tail_in1):
            prior = part[2 * ROWS :]
            flag = jnp.broadcast_to(prior[27:28], (ROWS, LANES))
            inverse_lumped = inverse_mass * (1.0 + 7.0 * flag)
            stiff = (1.0 - 0.5 * flag) * inverse_lumped * (1.0 / 6.0)
            result.append(
                (
                    part[:ROWS] * inverse_lumped,
                    part[ROWS : 2 * ROWS] * inverse_lumped,
                    time_step * stiff * (1.0 - prior * prior),
                    gradient_energy * stiff,
                    3.0 * prior * prior - 1.0,
                )
            )
        return result

    spread_ratio = 2.0
    half_width = 0.5
    weight_prev = 1.0 / spread_ratio
    update = [None] * blocks
    first_table, second_table = first_buf[...], second_buf[...]
    for sweep in range(SWEEPS):
        last = sweep == SWEEPS - 1
        product = jnp.dot(
            first_table, jnp.concatenate([split(v) for v in state], 1), preferred_element_type=F32
        )
        near = product[: 2 * ROWS]
        sources = [product[2 * ROWS :, b * LANES : (b + 1) * LANES] for b in range(blocks)]

        def pick(total, source, number, b):
            cols = slice(b * LANES, (b + 1) * LANES)
            index = index_buf[:, cols]
            got = jnp.take_along_axis(source, index, axis=1, mode="promise_in_bounds")
            return jnp.where(block_buf[:, cols] == number, got, total)

        faces = []
        for b in range(blocks):
            total = jnp.zeros((FACE_ROWS, LANES), F32)
            for number in range(blocks):
                total = pick(total, sources[number], number, b)
            faces.append(total)
        if sweep == 0:
            coefficients = coefficients_of()

        @pl.when(below[0])
        def _():
            up_copies[sweep].wait_recv()

        @pl.when(above[0])
        def _():
            down_copies[sweep].wait_recv()

        got_below, got_above = ghost_in[sweep, 0], ghost_in[sweep, 1]
        if sweep == 0:
            @pl.when(below_left[0])
            def _():
                corner_up.wait_recv()

            @pl.when(above_left[0])
            def _():
                corner_down.wait_recv()

            got_below = got_below + corner_in[0]
            got_above = got_above + corner_in[1]
        ghost = jnp.concatenate(
            [
                jnp.where(lane32 < HALF, got_below, pltpu.roll(got_above, HALF, 1)),
                jnp.where(lane32 < HALF, pltpu.roll(got_below, HALF, 1), got_above),
            ],
            0,
        )
        ghost_faces = jnp.dot(first_table[2 * ROWS :], split(ghost), preferred_element_type=F32)

        weight_now = 1.0 / (2.0 * spread_ratio - weight_prev)
        for b in range(blocks):
            total = pick(faces[b], ghost_faces, blocks, b)
            coupled = jnp.dot(second_table, split(total), preferred_element_type=F32)
            laplace = near[:, b * LANES : (b + 1) * LANES] + coupled
            side_c, side_mu, mobile, stiff, curvature = coefficients[b]
            c, mu = state[b][:ROWS], state[b][ROWS:]
            scaled = jnp.concatenate(
                [
                    side_c - c - mobile * laplace[ROWS:],
                    side_mu - mu + curvature * c + stiff * laplace[:ROWS],
                ],
                0,
            )
            if sweep == 0:
                update[b] = scaled
            else:
                update[b] = (
                    weight_now * weight_prev * update[b] + (2.0 * weight_now / half_width) * scaled
                )
            state[b] = state[b] + update[b]
            if last:
                out[pl.ds(2 * b, 27, stride=2 * blocks), :] = state[b][:27]
                out[pl.ds(2 * b + 1, 27, stride=2 * blocks), :] = state[b][ROWS : ROWS + 27]
            elif b == 0:
                send(sweep + 1, state[0][:ROWS], state[0][ROWS:])
        if sweep > 0:
            weight_prev = weight_now

    @pl.when(left[0])
    def _():
        for copy in head_copies:
            copy.wait_send()

    @pl.when(after[0])
    def _():
        for copy in tail_copies:
            copy.wait_send()

    @pl.when(above_after[0])
    def _():
        corner_up.wait_send()

    @pl.when(below_after[0])
    def _():
        corner_down.wait_send()

    for sweep in range(SWEEPS):
        @pl.when(above[0])
        def _():
            up_copies[sweep].wait_send()

        @pl.when(below[0])
        def _():
            down_copies[sweep].wait_send()


def local(n_seg, n_sub, start_state, right_side, previous, refined, old_cuts, new_cuts, face_links):
    capacity = start_state.shape[-1]
    first, second, inverse = element_tables()
    any_space = pl.BlockSpec(memory_space=pl.ANY)
    smem = pl.BlockSpec(memory_space=pltpu.SMEM)
    blocks = capacity // LANES

    def by_node(array):
        array = array.transpose(1, 0, 2).reshape(27, 2, blocks, LANES)
        return array.transpose(0, 2, 1, 3).reshape(54 * blocks, LANES)

    smoothed = pl.pallas_call(
        functools.partial(kernel, n_seg, n_sub),
        out_shape=pltpu.VMEM((54 * blocks, LANES), F32),
        in_specs=[smem, smem] + [any_space] * 8,
        out_specs=pl.BlockSpec(memory_space=pltpu.VMEM),
        scratch_shapes=[
            pltpu.VMEM((54 * blocks, LANES), F32),
            pltpu.VMEM((54 * blocks, LANES), F32),
            pltpu.VMEM((27, capacity), F32),
            pltpu.VMEM((1, capacity), jnp.int32),
            pltpu.VMEM((6, capacity), jnp.int32),
            pltpu.VMEM(first.shape, BF16),
            pltpu.VMEM(second.shape, BF16),
            pltpu.VMEM(inverse.shape, F32),
            pltpu.VMEM((FACE_ROWS, capacity), jnp.int32),
            pltpu.VMEM((FACE_ROWS, capacity), jnp.int32),
            *[pltpu.VMEM((ROWS, LANES), F32)] * 4,
            *[pltpu.VMEM((3 * ROWS // 2, LANES), F32)] * 4,
            pltpu.VMEM((SWEEPS, ROWS, LANES), F32),
            pltpu.VMEM((SWEEPS, 2, ROWS, LANES), F32),
            pltpu.VMEM((ROWS, LANES), F32),
            pltpu.VMEM((2, ROWS, LANES), F32),
            pltpu.VMEM((5 * ROWS, capacity), F32),
            pltpu.SemaphoreType.DMA((8,)),
            pltpu.SemaphoreType.DMA((2, 2)),
            pltpu.SemaphoreType.DMA((2, 2)),
            pltpu.SemaphoreType.DMA((SWEEPS, 2)),
            pltpu.SemaphoreType.DMA((SWEEPS, 2)),
            pltpu.SemaphoreType.DMA((2,)),
            pltpu.SemaphoreType.DMA((2,)),
        ],
        compiler_params=pltpu.CompilerParams(
            collective_id=0, has_side_effects=True, vmem_limit_bytes=60 * 1024 * 1024
        ),
        name="smooth",
    )(
        old_cuts, new_cuts, by_node(start_state), by_node(right_side), previous,
        refined.reshape(1, capacity),
        face_links, jnp.asarray(first, BF16), jnp.asarray(second, BF16), jnp.asarray(inverse, F32),
    )
    smoothed = smoothed.reshape(27, blocks, 2, LANES).transpose(2, 0, 1, 3)
    return smoothed.reshape(2, 27, capacity)


def solution(mesh):
    placed = (
        P(None, None, ("seg", "sub")),
        P(None, None, ("seg", "sub")),
        P(None, ("seg", "sub")),
        P(("seg", "sub")),
        P("seg", None),
        P("seg", None),
        P(None, ("seg", "sub")),
    )
    return jax.shard_map(
        functools.partial(local, mesh.shape["seg"], mesh.shape["sub"]),
        mesh=mesh, in_specs=placed, out_specs=P(None, None, ("seg", "sub")), check_vma=False,
    )
```

```python
import functools

import jax
import jax.numpy as jnp
import numpy as np
from jax import lax
from jax.experimental import pallas as pl
from jax.experimental.pallas import tpu as pltpu
from jax.sharding import PartitionSpec as P

SWEEPS = 3
MESH = pl.DeviceIdType.MESH
F32 = jnp.float32
BF16 = jnp.bfloat16
LANES = 128
HALF = 64
ROWS = 32
FACE_ROWS = 112

time_step = 0.01
gradient_energy = 0.01
penalty = 2.0


def element_tables():
    weights = np.array([0.5, 2.0, 0.5])
    slope_table = np.array([[7.0, -8.0, 1.0], [-8.0, 16.0, -8.0], [1.0, -8.0, 7.0]])
    diagonal = np.diag(weights)
    stiffness = (
        np.kron(slope_table, np.kron(diagonal, diagonal))
        + np.kron(diagonal, np.kron(slope_table, diagonal))
        + np.kron(diagonal, np.kron(diagonal, slope_table))
    )
    mass_table = np.kron(weights, np.kron(weights, weights))
    face_diag = np.zeros(27)
    select = np.zeros((FACE_ROWS, 2 * ROWS))
    scatter = np.zeros((2 * ROWS, FACE_ROWS))
    for direction in range(3):
        for side in range(2):
            surface = 2 * direction + side
            for major in range(3):
                for minor in range(3):
                    near = [major, minor]
                    near.insert(direction, 2 * side)
                    far = [major, minor]
                    far.insert(direction, 2 - 2 * side)
                    near_node = near[0] * 9 + near[1] * 3 + near[2]
                    far_node = far[0] * 9 + far[1] * 3 + far[2]
                    weight = weights[major] * weights[minor]
                    face_diag[near_node] += weight
                    for part in range(2):
                        row = surface * 18 + part * 9 + major * 3 + minor
                        select[row, part * ROWS + far_node] = -6.0 * penalty * weight
                        scatter[part * ROWS + near_node, row] = 1.0
    block = stiffness + 6.0 * penalty * np.diag(face_diag)
    local = np.zeros((2 * ROWS, 2 * ROWS))
    local[:27, :27] = block
    local[ROWS : ROWS + 27, ROWS : ROWS + 27] = block
    first = np.concatenate([local, select], 0)
    first = np.concatenate([first, first], 1)
    second = np.concatenate([scatter, scatter], 1)
    inverse = np.zeros((ROWS, LANES))
    inverse[:27] = 1.0 / mass_table[:, None]
    return first, second, inverse


def split(values):
    high = values.astype(BF16)
    low = (values - high.astype(F32)).astype(BF16)
    return jnp.concatenate([high, low], 0)


def kernel(
    n_seg, n_sub, old_cuts, new_cuts, start, right, prev, refined, links, first, second, inverse,
    out, state_buf, side_buf, prior_buf, flags, link_buf, first_buf, second_buf, inverse_buf,
    index_buf, block_buf, head_out0, tail_out0, head_in0, tail_in0,
    head_out1, tail_out1, head_in1, tail_in1, ghost_out, ghost_in,
    corner_out, corner_in, moved_buf, load_sem, head_sem, tail_sem, ghost_send, ghost_recv,
    corner_send, corner_recv,
):
    seg, sub = lax.axis_index("seg"), lax.axis_index("sub")
    capacity = links.shape[1]
    blocks = capacity // LANES

    loads = [
        pltpu.make_async_copy(source, target, load_sem.at[i])
        for i, (source, target) in enumerate(
            [
                (start, state_buf),
                (right, side_buf),
                (prev, prior_buf),
                (refined, flags),
                (links, link_buf),
                (first, first_buf),
                (second, second_buf),
                (inverse, inverse_buf),
            ]
        )
    ]
    for load in loads:
        load.start()

    for arriving in (head_in0, tail_in0, head_in1, tail_in1):
        arriving[...] = jnp.zeros_like(arriving)
    ghost_in[...] = jnp.zeros_like(ghost_in)
    corner_in[...] = jnp.zeros_like(corner_in)

    left = (sub > 0, (seg, sub - 1))
    after = (sub < n_sub - 1, (seg, sub + 1))
    below = (seg > 0, (seg - 1, sub))
    above = (seg < n_seg - 1, (seg + 1, sub))
    above_after = (above[0] & after[0], (seg + 1, sub + 1))
    below_after = (below[0] & after[0], (seg - 1, sub + 1))
    above_left = (above[0] & left[0], (seg + 1, sub - 1))
    below_left = (below[0] & left[0], (seg - 1, sub - 1))
    sides = (left, after, below, above, above_left, below_left)
    barrier = pltpu.get_barrier_semaphore()
    for there, place in sides:
        @pl.when(there)
        def _(place=place):
            pl.semaphore_signal(barrier, inc=1, device_id=place, device_id_type=MESH)

    head_copies = [
        pltpu.make_async_remote_copy(
            src_ref=source, dst_ref=target, send_sem=head_sem.at[i, 0], recv_sem=head_sem.at[i, 1],
            device_id=left[1], device_id_type=MESH)
        for i, (source, target) in enumerate([(head_out0, head_in0), (head_out1, head_in1)])
    ]
    tail_copies = [
        pltpu.make_async_remote_copy(
            src_ref=source, dst_ref=target, send_sem=tail_sem.at[i, 0], recv_sem=tail_sem.at[i, 1],
            device_id=after[1], device_id_type=MESH)
        for i, (source, target) in enumerate([(tail_out0, tail_in0), (tail_out1, tail_in1)])
    ]
    up_copies, down_copies = [], []
    for sweep in range(SWEEPS):
        up_copies.append(pltpu.make_async_remote_copy(
            src_ref=ghost_out.at[sweep], dst_ref=ghost_in.at[sweep, 0],
            send_sem=ghost_send.at[sweep, 0], recv_sem=ghost_recv.at[sweep, 0],
            device_id=above[1], device_id_type=MESH))
        down_copies.append(pltpu.make_async_remote_copy(
            src_ref=ghost_out.at[sweep], dst_ref=ghost_in.at[sweep, 1],
            send_sem=ghost_send.at[sweep, 1], recv_sem=ghost_recv.at[sweep, 1],
            device_id=below[1], device_id_type=MESH))

    corner_up = pltpu.make_async_remote_copy(
        src_ref=corner_out, dst_ref=corner_in.at[0], send_sem=corner_send.at[0],
        recv_sem=corner_recv.at[0], device_id=above_after[1], device_id_type=MESH)
    corner_down = pltpu.make_async_remote_copy(
        src_ref=corner_out, dst_ref=corner_in.at[1], send_sem=corner_send.at[1],
        recv_sem=corner_recv.at[1], device_id=below_after[1], device_id_type=MESH)

    old_first, old_end = old_cuts[0, sub], old_cuts[0, sub + 1]
    new_first, new_end = new_cuts[0, sub], new_cuts[0, sub + 1]
    left_first = old_cuts[0, jnp.maximum(sub - 1, 0)]
    old_count, new_count = old_end - old_first, new_end - new_first
    shift = new_first - old_first
    mask = LANES - 1
    lane = lax.broadcasted_iota(jnp.int32, (8, LANES), 1)
    row = lax.broadcasted_iota(jnp.int32, (8, LANES), 0)

    def wide(values, rows):
        return jnp.broadcast_to(values[:1], (rows, LANES))

    def lanes(rows):
        return lax.broadcasted_iota(jnp.int32, (rows, LANES), 1)

    pad = jnp.zeros((ROWS - 27, LANES), F32)
    row32 = lax.broadcasted_iota(jnp.int32, (ROWS, LANES), 0)

    def component(buffer, b, part):
        rows = buffer[pl.ds(2 * b + part, 27, stride=2 * blocks), :]
        return jnp.concatenate([rows, pad], 0)

    def pack_edges(whole, head_out, tail_out):
        count = whole[0].shape[0]
        upper = count // 2
        lane_u, lane_a = lanes(upper), lanes(count)
        head_out[...] = jnp.where(
            lane_u < HALF, whole[0][:upper], pltpu.roll(whole[0][upper:], HALF, 1)
        )
        tail = whole[0]
        window = (lane_u >= old_count - HALF) & (lane_u < old_count)
        for b in range(1, blocks):
            slot = lane_a + b * LANES
            inside = (slot >= old_count - HALF) & (slot < old_count)
            tail = jnp.where(inside, whole[b], tail)
            slot_u = lane_u + b * LANES
            window = window | ((slot_u >= old_count - HALF) & (slot_u < old_count))
        tail_out[...] = jnp.where(window, tail[:upper], pltpu.roll(tail[upper:], HALF, 1))
        return tail

    def start_edges(i):
        @pl.when(after[0])
        def _():
            tail_copies[i].start()

        @pl.when(left[0])
        def _():
            head_copies[i].start()

    def rotate(whole, first_row):
        turned = [pltpu.roll(w, turn, 1) for w in whole]
        came_from = lanes(whole[0].shape[0]) + shift
        for b in range(blocks):
            mine = turned[b]
            if b > 0:
                mine = jnp.where(came_from < 0, turned[b - 1], mine)
            if b < blocks - 1:
                mine = jnp.where(came_from >= LANES, turned[b + 1], mine)
            rows = slice(first_row, first_row + whole[0].shape[0])
            moved_buf[rows, b * LANES : (b + 1) * LANES] = mine

    def from_edge(arrived, amount):
        return jnp.concatenate(
            [
                pltpu.roll(arrived[...], amount & mask, 1),
                pltpu.roll(arrived[...], (amount + HALF) & mask, 1),
            ],
            0,
        )

    edge = old_end - new_first

    def arrive(i, first_row, count, head_in, tail_in):
        @pl.when(left[0])
        def _():
            tail_copies[i].wait_recv()

        @pl.when(after[0])
        def _():
            head_copies[i].wait_recv()

        from_left = from_edge(tail_in, left_first - new_first)
        from_right = from_edge(head_in, edge)
        lane_a = lanes(count)
        result = []
        for b in range(blocks):
            slot = lane_a + b * LANES
            part = moved_buf[first_row : first_row + count, b * LANES : (b + 1) * LANES]
            if b == 0:
                part = jnp.where(slot < -shift, from_left, part)
            part = jnp.where(slot >= edge, from_right, part)
            result.append(jnp.where(slot < new_count, part, 0.0))
        return result

    loads[0].wait()
    whole = [
        jnp.concatenate([component(state_buf, b, 0), component(state_buf, b, 1)], 0)
        for b in range(blocks)
    ]
    turn = (-shift) & mask
    lane32 = lanes(ROWS)
    slot32 = lane32 & (HALF - 1)

    def both(rows, amount):
        return jnp.where(
            lane32 < HALF,
            pltpu.roll(rows[:ROWS], amount & mask, 1),
            pltpu.roll(rows[ROWS : 2 * ROWS], (amount + HALF) & mask, 1),
        )

    ghost_out[0] = jnp.where(
        (slot32 >= -shift) & (slot32 < new_count), both(whole[0], turn), 0.0
    )
    seg_sides = jnp.minimum(seg, 1) + jnp.minimum(n_seg - 1 - seg, 1)
    has_after = jnp.minimum(n_sub - 1 - sub, 1)
    pl.semaphore_wait(barrier, jnp.minimum(sub, 1) + has_after + seg_sides * (1 + has_after))

    for there, copy in ((above[0], up_copies[0]), (below[0], down_copies[0])
    ):
        @pl.when(there)
        def _(copy=copy):
            copy.start()

    tail = pack_edges(whole, head_out0, tail_out0)

    start_edges(0)

    next_count = new_cuts[0, jnp.minimum(sub + 2, n_sub)] - new_end
    corner_out[...] = jnp.where(
        (slot32 < old_end - new_end) & (slot32 < next_count), both(tail, old_first - new_end), 0.0
    )

    for there, copy in ((above_after[0], corner_up), (below_after[0], corner_down)
    ):
        @pl.when(there)
        def _(copy=copy):
            copy.start()

    for i in range(1, 4):
        loads[i].wait()
    others = []
    for b in range(blocks):
        cols = pl.ds(b * LANES, LANES)
        flag = flags[:, cols].astype(F32)
        prior = jnp.concatenate([prior_buf[:, cols], pad], 0)
        prior = jnp.where(row32 == 27, jnp.broadcast_to(flag, (ROWS, LANES)), prior)
        others.append(
            jnp.concatenate([component(side_buf, b, 0), component(side_buf, b, 1), prior], 0)
        )
    pack_edges(others, head_out1, tail_out1)
    start_edges(1)
    rotate(whole, 0)

    loads[4].wait()
    for b in range(blocks):
        cols = pl.ds(b * LANES, LANES)
        rows = [jnp.broadcast_to(link_buf[f : f + 1, cols], (8, LANES)) for f in range(6)]
        parts = []
        for k in range(FACE_ROWS // 8):
            f0, f1 = min(8 * k // 18, 5), min((8 * k + 7) // 18, 5)
            part = rows[f0]
            if f1 != f0:
                part = jnp.where(row < f1 * 18 - 8 * k, part, rows[f1])
            parts.append(part)
        link = jnp.concatenate(parts, 0)
        index_buf[:, cols] = link & mask
        block_buf[:, cols] = link >> 7
    for i in range(5, 8):
        loads[i].wait()

    def send(sweep, c, mu):
        ghost_out[sweep] = jnp.where(lane32 < HALF, c, pltpu.roll(mu, HALF, 1))

        @pl.when(above[0])
        def _():
            up_copies[sweep].start()

        @pl.when(below[0])
        def _():
            down_copies[sweep].start()

    state = arrive(0, 0, 2 * ROWS, head_in0, tail_in0)
    rotate(others, 2 * ROWS)

    def coefficients_of():
        result = []
        inverse_mass = inverse_buf[...]
        for part in arrive(1, 2 * ROWS, 3 * ROWS, head_in1, tail_in1):
            prior = part[2 * ROWS :]
            flag = jnp.broadcast_to(prior[27:28], (ROWS, LANES))
            inverse_lumped = inverse_mass * (1.0 + 7.0 * flag)
            stiff = (1.0 - 0.5 * flag) * inverse_lumped * (1.0 / 6.0)
            result.append(
                (
                    part[:ROWS] * inverse_lumped,
                    part[ROWS : 2 * ROWS] * inverse_lumped,
                    time_step * stiff * (1.0 - prior * prior),
                    gradient_energy * stiff,
                    3.0 * prior * prior - 1.0,
                )
            )
        return result

    spread_ratio = 2.0
    half_width = 0.5
    weight_prev = 1.0 / spread_ratio
    update = [None] * blocks
    first_table, second_table = first_buf[...], second_buf[...]
    for sweep in range(SWEEPS):
        last = sweep == SWEEPS - 1
        product = jnp.dot(
            first_table, jnp.concatenate([split(v) for v in state], 1), preferred_element_type=F32
        )
        near = product[: 2 * ROWS]
        sources = [product[2 * ROWS :, b * LANES : (b + 1) * LANES] for b in range(blocks)]

        def pick(total, source, number, b):
            cols = slice(b * LANES, (b + 1) * LANES)
            index = index_buf[:, cols]
            got = jnp.take_along_axis(source, index, axis=1, mode="promise_in_bounds")
            return jnp.where(block_buf[:, cols] == number, got, total)

        faces = []
        for b in range(blocks):
            total = jnp.zeros((FACE_ROWS, LANES), F32)
            for number in range(blocks):
                total = pick(total, sources[number], number, b)
            faces.append(total)
        if sweep == 0:
            coefficients = coefficients_of()

        @pl.when(below[0])
        def _():
            up_copies[sweep].wait_recv()

        @pl.when(above[0])
        def _():
            down_copies[sweep].wait_recv()

        got_below, got_above = ghost_in[sweep, 0], ghost_in[sweep, 1]
        if sweep == 0:
            @pl.when(below_left[0])
            def _():
                corner_up.wait_recv()

            @pl.when(above_left[0])
            def _():
                corner_down.wait_recv()

            got_below = got_below + corner_in[0]
            got_above = got_above + corner_in[1]
        ghost = jnp.concatenate(
            [
                jnp.where(lane32 < HALF, got_below, pltpu.roll(got_above, HALF, 1)),
                jnp.where(lane32 < HALF, pltpu.roll(got_below, HALF, 1), got_above),
            ],
            0,
        )
        ghost_faces = jnp.dot(first_table[2 * ROWS :], split(ghost), preferred_element_type=F32)

        weight_now = 1.0 / (2.0 * spread_ratio - weight_prev)
        for b in range(blocks):
            total = pick(faces[b], ghost_faces, blocks, b)
            coupled = jnp.dot(second_table, split(total), preferred_element_type=F32)
            laplace = near[:, b * LANES : (b + 1) * LANES] + coupled
            side_c, side_mu, mobile, stiff, curvature = coefficients[b]
            c, mu = state[b][:ROWS], state[b][ROWS:]
            scaled = jnp.concatenate(
                [
                    side_c - c - mobile * laplace[ROWS:],
                    side_mu - mu + curvature * c + stiff * laplace[:ROWS],
                ],
                0,
            )
            if sweep == 0:
                update[b] = scaled
            else:
                update[b] = (
                    weight_now * weight_prev * update[b] + (2.0 * weight_now / half_width) * scaled
                )
            state[b] = state[b] + update[b]
            if last:
                out[pl.ds(2 * b, 27, stride=2 * blocks), :] = state[b][:27]
                out[pl.ds(2 * b + 1, 27, stride=2 * blocks), :] = state[b][ROWS : ROWS + 27]
            elif b == 0:
                send(sweep + 1, state[0][:ROWS], state[0][ROWS:])
        if sweep > 0:
            weight_prev = weight_now

    @pl.when(left[0])
    def _():
        for copy in head_copies:
            copy.wait_send()

    @pl.when(after[0])
    def _():
        for copy in tail_copies:
            copy.wait_send()

    @pl.when(above_after[0])
    def _():
        corner_up.wait_send()

    @pl.when(below_after[0])
    def _():
        corner_down.wait_send()

    for sweep in range(SWEEPS):
        @pl.when(above[0])
        def _():
            up_copies[sweep].wait_send()

        @pl.when(below[0])
        def _():
            down_copies[sweep].wait_send()


def local(n_seg, n_sub, start_state, right_side, previous, refined, old_cuts, new_cuts, face_links):
    capacity = start_state.shape[-1]
    first, second, inverse = element_tables()
    any_space = pl.BlockSpec(memory_space=pl.ANY)
    smem = pl.BlockSpec(memory_space=pltpu.SMEM)
    blocks = capacity // LANES

    def by_node(array):
        array = array.transpose(1, 0, 2).reshape(27, 2, blocks, LANES)
        return array.transpose(0, 2, 1, 3).reshape(54 * blocks, LANES)

    smoothed = pl.pallas_call(
        functools.partial(kernel, n_seg, n_sub),
        out_shape=pltpu.VMEM((54 * blocks, LANES), F32),
        in_specs=[smem, smem] + [any_space] * 8,
        out_specs=pl.BlockSpec(memory_space=pltpu.VMEM),
        scratch_shapes=[
            pltpu.VMEM((54 * blocks, LANES), F32),
            pltpu.VMEM((54 * blocks, LANES), F32),
            pltpu.VMEM((27, capacity), F32),
            pltpu.VMEM((1, capacity), jnp.int32),
            pltpu.VMEM((6, capacity), jnp.int32),
            pltpu.VMEM(first.shape, BF16),
            pltpu.VMEM(second.shape, BF16),
            pltpu.VMEM(inverse.shape, F32),
            pltpu.VMEM((FACE_ROWS, capacity), jnp.int32),
            pltpu.VMEM((FACE_ROWS, capacity), jnp.int32),
            *[pltpu.VMEM((ROWS, LANES), F32)] * 4,
            *[pltpu.VMEM((3 * ROWS // 2, LANES), F32)] * 4,
            pltpu.VMEM((SWEEPS, ROWS, LANES), F32),
            pltpu.VMEM((SWEEPS, 2, ROWS, LANES), F32),
            pltpu.VMEM((ROWS, LANES), F32),
            pltpu.VMEM((2, ROWS, LANES), F32),
            pltpu.VMEM((5 * ROWS, capacity), F32),
            pltpu.SemaphoreType.DMA((8,)),
            pltpu.SemaphoreType.DMA((2, 2)),
            pltpu.SemaphoreType.DMA((2, 2)),
            pltpu.SemaphoreType.DMA((SWEEPS, 2)),
            pltpu.SemaphoreType.DMA((SWEEPS, 2)),
            pltpu.SemaphoreType.DMA((2,)),
            pltpu.SemaphoreType.DMA((2,)),
        ],
        compiler_params=pltpu.CompilerParams(
            collective_id=0, has_side_effects=True, vmem_limit_bytes=60 * 1024 * 1024
        ),
        name="smooth",
    )(
        old_cuts, new_cuts, by_node(start_state), by_node(right_side), previous,
        refined.reshape(1, capacity),
        face_links, jnp.asarray(first, BF16), jnp.asarray(second, BF16), jnp.asarray(inverse, F32),
    )
    smoothed = smoothed.reshape(27, blocks, 2, LANES).transpose(2, 0, 1, 3)
    return smoothed.reshape(2, 27, capacity)


def solution(mesh):
    placed = (
        P(None, None, ("seg", "sub")),
        P(None, None, ("seg", "sub")),
        P(None, ("seg", "sub")),
        P(("seg", "sub")),
        P("seg", None),
        P("seg", None),
        P(None, ("seg", "sub")),
    )
    return jax.shard_map(
        functools.partial(local, mesh.shape["seg"], mesh.shape["sub"]),
        mesh=mesh, in_specs=placed, out_specs=P(None, None, ("seg", "sub")), check_vma=False,
    )
```

```python
import functools

import jax
import jax.numpy as jnp
import numpy as np
from jax import lax
from jax.experimental import pallas as pl
from jax.experimental.pallas import tpu as pltpu
from jax.sharding import PartitionSpec as P

SWEEPS = 3
MESH = pl.DeviceIdType.MESH
F32 = jnp.float32
BF16 = jnp.bfloat16
LANES = 128
HALF = 64
ROWS = 32
FACE_ROWS = 112

time_step = 0.01
gradient_energy = 0.01
penalty = 2.0


def element_tables():
    weights = np.array([0.5, 2.0, 0.5])
    slope_table = np.array([[7.0, -8.0, 1.0], [-8.0, 16.0, -8.0], [1.0, -8.0, 7.0]])
    diagonal = np.diag(weights)
    stiffness = (
        np.kron(slope_table, np.kron(diagonal, diagonal))
        + np.kron(diagonal, np.kron(slope_table, diagonal))
        + np.kron(diagonal, np.kron(diagonal, slope_table))
    )
    mass_table = np.kron(weights, np.kron(weights, weights))
    face_diag = np.zeros(27)
    select = np.zeros((FACE_ROWS, 2 * ROWS))
    scatter = np.zeros((2 * ROWS, FACE_ROWS))
    for direction in range(3):
        for side in range(2):
            surface = 2 * direction + side
            for major in range(3):
                for minor in range(3):
                    near = [major, minor]
                    near.insert(direction, 2 * side)
                    far = [major, minor]
                    far.insert(direction, 2 - 2 * side)
                    near_node = near[0] * 9 + near[1] * 3 + near[2]
                    far_node = far[0] * 9 + far[1] * 3 + far[2]
                    weight = weights[major] * weights[minor]
                    face_diag[near_node] += weight
                    for part in range(2):
                        row = surface * 18 + part * 9 + major * 3 + minor
                        select[row, part * ROWS + far_node] = -6.0 * penalty * weight
                        scatter[part * ROWS + near_node, row] = 1.0
    block = stiffness + 6.0 * penalty * np.diag(face_diag)
    local = np.zeros((2 * ROWS, 2 * ROWS))
    local[:27, :27] = block
    local[ROWS : ROWS + 27, ROWS : ROWS + 27] = block
    first = np.concatenate([local, select], 0)
    first = np.concatenate([first, first], 1)
    second = np.concatenate([scatter, scatter], 1)
    inverse = np.zeros((ROWS, LANES))
    inverse[:27] = 1.0 / mass_table[:, None]
    return first, second, inverse


def split(values):
    high = values.astype(BF16)
    low = (values - high.astype(F32)).astype(BF16)
    return jnp.concatenate([high, low], 0)


def kernel(
    n_seg, n_sub, old_cuts, new_cuts, start, right, prev, refined, links, first, second, inverse,
    out, state_buf, side_buf, prior_buf, flags, link_buf, first_buf, second_buf, inverse_buf,
    index_buf, block_buf, head_out0, tail_out0, head_in0, tail_in0,
    head_out1, tail_out1, head_in1, tail_in1, ghost_out, ghost_in,
    corner_out, corner_in, moved_buf, load_sem, head_sem, tail_sem, ghost_send, ghost_recv,
    corner_send, corner_recv,
):
    seg, sub = lax.axis_index("seg"), lax.axis_index("sub")
    capacity = links.shape[1]
    blocks = capacity // LANES

    loads = [
        pltpu.make_async_copy(source, target, load_sem.at[i])
        for i, (source, target) in enumerate(
            [
                (start, state_buf),
                (right, side_buf),
                (prev, prior_buf),
                (refined, flags),
                (links, link_buf),
                (first, first_buf),
                (second, second_buf),
                (inverse, inverse_buf),
            ]
        )
    ]
    loads[0].start()

    for arriving in (head_in0, tail_in0, head_in1, tail_in1):
        arriving[...] = jnp.zeros_like(arriving)
    ghost_in[...] = jnp.zeros_like(ghost_in)
    corner_in[...] = jnp.zeros_like(corner_in)

    left = (sub > 0, (seg, sub - 1))
    after = (sub < n_sub - 1, (seg, sub + 1))
    below = (seg > 0, (seg - 1, sub))
    above = (seg < n_seg - 1, (seg + 1, sub))
    above_after = (above[0] & after[0], (seg + 1, sub + 1))
    below_after = (below[0] & after[0], (seg - 1, sub + 1))
    above_left = (above[0] & left[0], (seg + 1, sub - 1))
    below_left = (below[0] & left[0], (seg - 1, sub - 1))
    sides = (left, after, below, above, above_left, below_left)
    barrier = pltpu.get_barrier_semaphore()
    for there, place in sides:
        @pl.when(there)
        def _(place=place):
            pl.semaphore_signal(barrier, inc=1, device_id=place, device_id_type=MESH)
    for load in loads[1:]:
        load.start()

    head_copies = [
        pltpu.make_async_remote_copy(
            src_ref=source, dst_ref=target, send_sem=head_sem.at[i, 0], recv_sem=head_sem.at[i, 1],
            device_id=left[1], device_id_type=MESH)
        for i, (source, target) in enumerate([(head_out0, head_in0), (head_out1, head_in1)])
    ]
    tail_copies = [
        pltpu.make_async_remote_copy(
            src_ref=source, dst_ref=target, send_sem=tail_sem.at[i, 0], recv_sem=tail_sem.at[i, 1],
            device_id=after[1], device_id_type=MESH)
        for i, (source, target) in enumerate([(tail_out0, tail_in0), (tail_out1, tail_in1)])
    ]
    up_copies, down_copies = [], []
    for sweep in range(SWEEPS):
        up_copies.append(pltpu.make_async_remote_copy(
            src_ref=ghost_out.at[sweep], dst_ref=ghost_in.at[sweep, 0],
            send_sem=ghost_send.at[sweep, 0], recv_sem=ghost_recv.at[sweep, 0],
            device_id=above[1], device_id_type=MESH))
        down_copies.append(pltpu.make_async_remote_copy(
            src_ref=ghost_out.at[sweep], dst_ref=ghost_in.at[sweep, 1],
            send_sem=ghost_send.at[sweep, 1], recv_sem=ghost_recv.at[sweep, 1],
            device_id=below[1], device_id_type=MESH))

    corner_up = pltpu.make_async_remote_copy(
        src_ref=corner_out, dst_ref=corner_in.at[0], send_sem=corner_send.at[0],
        recv_sem=corner_recv.at[0], device_id=above_after[1], device_id_type=MESH)
    corner_down = pltpu.make_async_remote_copy(
        src_ref=corner_out, dst_ref=corner_in.at[1], send_sem=corner_send.at[1],
        recv_sem=corner_recv.at[1], device_id=below_after[1], device_id_type=MESH)

    old_first, old_end = old_cuts[0, sub], old_cuts[0, sub + 1]
    new_first, new_end = new_cuts[0, sub], new_cuts[0, sub + 1]
    left_first = old_cuts[0, jnp.maximum(sub - 1, 0)]
    old_count, new_count = old_end - old_first, new_end - new_first
    shift = new_first - old_first
    mask = LANES - 1
    lane = lax.broadcasted_iota(jnp.int32, (8, LANES), 1)
    row = lax.broadcasted_iota(jnp.int32, (8, LANES), 0)

    def wide(values, rows):
        return jnp.broadcast_to(values[:1], (rows, LANES))

    def lanes(rows):
        return lax.broadcasted_iota(jnp.int32, (rows, LANES), 1)

    pad = jnp.zeros((ROWS - 27, LANES), F32)
    row32 = lax.broadcasted_iota(jnp.int32, (ROWS, LANES), 0)

    def component(buffer, b, part):
        rows = buffer[pl.ds(2 * b + part, 27, stride=2 * blocks), :]
        return jnp.concatenate([rows, pad], 0)

    def pack_edges(whole, head_out, tail_out):
        count = whole[0].shape[0]
        upper = count // 2
        lane_u, lane_a = lanes(upper), lanes(count)
        head_out[...] = jnp.where(
            lane_u < HALF, whole[0][:upper], pltpu.roll(whole[0][upper:], HALF, 1)
        )
        tail = whole[0]
        window = (lane_u >= old_count - HALF) & (lane_u < old_count)
        for b in range(1, blocks):
            slot = lane_a + b * LANES
            inside = (slot >= old_count - HALF) & (slot < old_count)
            tail = jnp.where(inside, whole[b], tail)
            slot_u = lane_u + b * LANES
            window = window | ((slot_u >= old_count - HALF) & (slot_u < old_count))
        tail_out[...] = jnp.where(window, tail[:upper], pltpu.roll(tail[upper:], HALF, 1))
        return tail

    def start_edges(i):
        @pl.when(after[0])
        def _():
            tail_copies[i].start()

        @pl.when(left[0])
        def _():
            head_copies[i].start()

    def rotate(whole, first_row):
        turned = [pltpu.roll(w, turn, 1) for w in whole]
        came_from = lanes(whole[0].shape[0]) + shift
        for b in range(blocks):
            mine = turned[b]
            if b > 0:
                mine = jnp.where(came_from < 0, turned[b - 1], mine)
            if b < blocks - 1:
                mine = jnp.where(came_from >= LANES, turned[b + 1], mine)
            rows = slice(first_row, first_row + whole[0].shape[0])
            moved_buf[rows, b * LANES : (b + 1) * LANES] = mine

    def from_edge(arrived, amount):
        return jnp.concatenate(
            [
                pltpu.roll(arrived[...], amount & mask, 1),
                pltpu.roll(arrived[...], (amount + HALF) & mask, 1),
            ],
            0,
        )

    edge = old_end - new_first

    def arrive(i, first_row, count, head_in, tail_in):
        @pl.when(left[0])
        def _():
            tail_copies[i].wait_recv()

        @pl.when(after[0])
        def _():
            head_copies[i].wait_recv()

        from_left = from_edge(tail_in, left_first - new_first)
        from_right = from_edge(head_in, edge)
        lane_a = lanes(count)
        result = []
        for b in range(blocks):
            slot = lane_a + b * LANES
            part = moved_buf[first_row : first_row + count, b * LANES : (b + 1) * LANES]
            if b == 0:
                part = jnp.where(slot < -shift, from_left, part)
            part = jnp.where(slot >= edge, from_right, part)
            result.append(jnp.where(slot < new_count, part, 0.0))
        return result

    loads[0].wait()
    whole = [
        jnp.concatenate([component(state_buf, b, 0), component(state_buf, b, 1)], 0)
        for b in range(blocks)
    ]
    turn = (-shift) & mask
    lane32 = lanes(ROWS)
    slot32 = lane32 & (HALF - 1)

    def both(rows, amount):
        return jnp.where(
            lane32 < HALF,
            pltpu.roll(rows[:ROWS], amount & mask, 1),
            pltpu.roll(rows[ROWS : 2 * ROWS], (amount + HALF) & mask, 1),
        )

    ghost_out[0] = jnp.where(
        (slot32 >= -shift) & (slot32 < new_count), both(whole[0], turn), 0.0
    )
    seg_sides = jnp.minimum(seg, 1) + jnp.minimum(n_seg - 1 - seg, 1)
    has_after = jnp.minimum(n_sub - 1 - sub, 1)
    pl.semaphore_wait(barrier, jnp.minimum(sub, 1) + has_after + seg_sides * (1 + has_after))

    for there, copy in ((above[0], up_copies[0]), (below[0], down_copies[0])
    ):
        @pl.when(there)
        def _(copy=copy):
            copy.start()

    tail = pack_edges(whole, head_out0, tail_out0)

    start_edges(0)

    next_count = new_cuts[0, jnp.minimum(sub + 2, n_sub)] - new_end
    corner_out[...] = jnp.where(
        (slot32 < old_end - new_end) & (slot32 < next_count), both(tail, old_first - new_end), 0.0
    )

    for there, copy in ((above_after[0], corner_up), (below_after[0], corner_down)
    ):
        @pl.when(there)
        def _(copy=copy):
            copy.start()

    for i in range(1, 4):
        loads[i].wait()
    others = []
    for b in range(blocks):
        cols = pl.ds(b * LANES, LANES)
        flag = flags[:, cols].astype(F32)
        prior = jnp.concatenate([prior_buf[:, cols], pad], 0)
        prior = jnp.where(row32 == 27, jnp.broadcast_to(flag, (ROWS, LANES)), prior)
        others.append(
            jnp.concatenate([component(side_buf, b, 0), component(side_buf, b, 1), prior], 0)
        )
    pack_edges(others, head_out1, tail_out1)
    start_edges(1)
    rotate(whole, 0)

    loads[4].wait()
    for b in range(blocks):
        cols = pl.ds(b * LANES, LANES)
        rows = [jnp.broadcast_to(link_buf[f : f + 1, cols], (8, LANES)) for f in range(6)]
        parts = []
        for k in range(FACE_ROWS // 8):
            f0, f1 = min(8 * k // 18, 5), min((8 * k + 7) // 18, 5)
            part = rows[f0]
            if f1 != f0:
                part = jnp.where(row < f1 * 18 - 8 * k, part, rows[f1])
            parts.append(part)
        link = jnp.concatenate(parts, 0)
        index_buf[:, cols] = link & mask
        block_buf[:, cols] = link >> 7
    for i in range(5, 8):
        loads[i].wait()

    def send(sweep, c, mu):
        ghost_out[sweep] = jnp.where(lane32 < HALF, c, pltpu.roll(mu, HALF, 1))

        @pl.when(above[0])
        def _():
            up_copies[sweep].start()

        @pl.when(below[0])
        def _():
            down_copies[sweep].start()

    state = arrive(0, 0, 2 * ROWS, head_in0, tail_in0)
    rotate(others, 2 * ROWS)

    def coefficients_of():
        result = []
        inverse_mass = inverse_buf[...]
        for part in arrive(1, 2 * ROWS, 3 * ROWS, head_in1, tail_in1):
            prior = part[2 * ROWS :]
            flag = jnp.broadcast_to(prior[27:28], (ROWS, LANES))
            inverse_lumped = inverse_mass * (1.0 + 7.0 * flag)
            stiff = (1.0 - 0.5 * flag) * inverse_lumped * (1.0 / 6.0)
            result.append(
                (
                    part[:ROWS] * inverse_lumped,
                    part[ROWS : 2 * ROWS] * inverse_lumped,
                    time_step * stiff * (1.0 - prior * prior),
                    gradient_energy * stiff,
                    3.0 * prior * prior - 1.0,
                )
            )
        return result

    spread_ratio = 2.0
    half_width = 0.5
    weight_prev = 1.0 / spread_ratio
    update = [None] * blocks
    first_table, second_table = first_buf[...], second_buf[...]
    for sweep in range(SWEEPS):
        last = sweep == SWEEPS - 1
        product = jnp.dot(
            first_table, jnp.concatenate([split(v) for v in state], 1), preferred_element_type=F32
        )
        near = product[: 2 * ROWS]
        sources = [product[2 * ROWS :, b * LANES : (b + 1) * LANES] for b in range(blocks)]

        def pick(total, source, number, b):
            cols = slice(b * LANES, (b + 1) * LANES)
            index = index_buf[:, cols]
            got = jnp.take_along_axis(source, index, axis=1, mode="promise_in_bounds")
            return jnp.where(block_buf[:, cols] == number, got, total)

        faces = []
        for b in range(blocks):
            total = jnp.zeros((FACE_ROWS, LANES), F32)
            for number in range(blocks):
                total = pick(total, sources[number], number, b)
            faces.append(total)
        if sweep == 0:
            coefficients = coefficients_of()

        @pl.when(below[0])
        def _():
            up_copies[sweep].wait_recv()

        @pl.when(above[0])
        def _():
            down_copies[sweep].wait_recv()

        got_below, got_above = ghost_in[sweep, 0], ghost_in[sweep, 1]
        if sweep == 0:
            @pl.when(below_left[0])
            def _():
                corner_up.wait_recv()

            @pl.when(above_left[0])
            def _():
                corner_down.wait_recv()

            got_below = got_below + corner_in[0]
            got_above = got_above + corner_in[1]
        ghost = jnp.concatenate(
            [
                jnp.where(lane32 < HALF, got_below, pltpu.roll(got_above, HALF, 1)),
                jnp.where(lane32 < HALF, pltpu.roll(got_below, HALF, 1), got_above),
            ],
            0,
        )
        ghost_faces = jnp.dot(first_table[2 * ROWS :], split(ghost), preferred_element_type=F32)

        weight_now = 1.0 / (2.0 * spread_ratio - weight_prev)
        for b in range(blocks):
            total = pick(faces[b], ghost_faces, blocks, b)
            coupled = jnp.dot(second_table, split(total), preferred_element_type=F32)
            laplace = near[:, b * LANES : (b + 1) * LANES] + coupled
            side_c, side_mu, mobile, stiff, curvature = coefficients[b]
            c, mu = state[b][:ROWS], state[b][ROWS:]
            scaled = jnp.concatenate(
                [
                    side_c - c - mobile * laplace[ROWS:],
                    side_mu - mu + curvature * c + stiff * laplace[:ROWS],
                ],
                0,
            )
            if sweep == 0:
                update[b] = scaled
            else:
                update[b] = (
                    weight_now * weight_prev * update[b] + (2.0 * weight_now / half_width) * scaled
                )
            state[b] = state[b] + update[b]
            if last:
                out[pl.ds(2 * b, 27, stride=2 * blocks), :] = state[b][:27]
                out[pl.ds(2 * b + 1, 27, stride=2 * blocks), :] = state[b][ROWS : ROWS + 27]
            elif b == 0:
                send(sweep + 1, state[0][:ROWS], state[0][ROWS:])
        if sweep > 0:
            weight_prev = weight_now

    @pl.when(left[0])
    def _():
        for copy in head_copies:
            copy.wait_send()

    @pl.when(after[0])
    def _():
        for copy in tail_copies:
            copy.wait_send()

    @pl.when(above_after[0])
    def _():
        corner_up.wait_send()

    @pl.when(below_after[0])
    def _():
        corner_down.wait_send()

    for sweep in range(SWEEPS):
        @pl.when(above[0])
        def _():
            up_copies[sweep].wait_send()

        @pl.when(below[0])
        def _():
            down_copies[sweep].wait_send()


def local(n_seg, n_sub, start_state, right_side, previous, refined, old_cuts, new_cuts, face_links):
    capacity = start_state.shape[-1]
    first, second, inverse = element_tables()
    any_space = pl.BlockSpec(memory_space=pl.ANY)
    smem = pl.BlockSpec(memory_space=pltpu.SMEM)
    blocks = capacity // LANES

    def by_node(array):
        array = array.transpose(1, 0, 2).reshape(27, 2, blocks, LANES)
        return array.transpose(0, 2, 1, 3).reshape(54 * blocks, LANES)

    smoothed = pl.pallas_call(
        functools.partial(kernel, n_seg, n_sub),
        out_shape=pltpu.VMEM((54 * blocks, LANES), F32),
        in_specs=[smem, smem] + [any_space] * 8,
        out_specs=pl.BlockSpec(memory_space=pltpu.VMEM),
        scratch_shapes=[
            pltpu.VMEM((54 * blocks, LANES), F32),
            pltpu.VMEM((54 * blocks, LANES), F32),
            pltpu.VMEM((27, capacity), F32),
            pltpu.VMEM((1, capacity), jnp.int32),
            pltpu.VMEM((6, capacity), jnp.int32),
            pltpu.VMEM(first.shape, BF16),
            pltpu.VMEM(second.shape, BF16),
            pltpu.VMEM(inverse.shape, F32),
            pltpu.VMEM((FACE_ROWS, capacity), jnp.int32),
            pltpu.VMEM((FACE_ROWS, capacity), jnp.int32),
            *[pltpu.VMEM((ROWS, LANES), F32)] * 4,
            *[pltpu.VMEM((3 * ROWS // 2, LANES), F32)] * 4,
            pltpu.VMEM((SWEEPS, ROWS, LANES), F32),
            pltpu.VMEM((SWEEPS, 2, ROWS, LANES), F32),
            pltpu.VMEM((ROWS, LANES), F32),
            pltpu.VMEM((2, ROWS, LANES), F32),
            pltpu.VMEM((5 * ROWS, capacity), F32),
            pltpu.SemaphoreType.DMA((8,)),
            pltpu.SemaphoreType.DMA((2, 2)),
            pltpu.SemaphoreType.DMA((2, 2)),
            pltpu.SemaphoreType.DMA((SWEEPS, 2)),
            pltpu.SemaphoreType.DMA((SWEEPS, 2)),
            pltpu.SemaphoreType.DMA((2,)),
            pltpu.SemaphoreType.DMA((2,)),
        ],
        compiler_params=pltpu.CompilerParams(
            collective_id=0, has_side_effects=True, vmem_limit_bytes=60 * 1024 * 1024
        ),
        name="smooth",
    )(
        old_cuts, new_cuts, by_node(start_state), by_node(right_side), previous,
        refined.reshape(1, capacity),
        face_links, jnp.asarray(first, BF16), jnp.asarray(second, BF16), jnp.asarray(inverse, F32),
    )
    smoothed = smoothed.reshape(27, blocks, 2, LANES).transpose(2, 0, 1, 3)
    return smoothed.reshape(2, 27, capacity)


def solution(mesh):
    placed = (
        P(None, None, ("seg", "sub")),
        P(None, None, ("seg", "sub")),
        P(None, ("seg", "sub")),
        P(("seg", "sub")),
        P("seg", None),
        P("seg", None),
        P(None, ("seg", "sub")),
    )
    return jax.shard_map(
        functools.partial(local, mesh.shape["seg"], mesh.shape["sub"]),
        mesh=mesh, in_specs=placed, out_specs=P(None, None, ("seg", "sub")), check_vma=False,
    )
```

```python
import functools

import jax
import jax.numpy as jnp
import numpy as np
from jax import lax
from jax.experimental import pallas as pl
from jax.experimental.pallas import tpu as pltpu
from jax.sharding import PartitionSpec as P

SWEEPS = 3
MESH = pl.DeviceIdType.MESH
F32 = jnp.float32
BF16 = jnp.bfloat16
LANES = 128
HALF = 64
ROWS = 32
FACE_ROWS = 112

time_step = 0.01
gradient_energy = 0.01
penalty = 2.0


def element_tables():
    weights = np.array([0.5, 2.0, 0.5])
    slope_table = np.array([[7.0, -8.0, 1.0], [-8.0, 16.0, -8.0], [1.0, -8.0, 7.0]])
    diagonal = np.diag(weights)
    stiffness = (
        np.kron(slope_table, np.kron(diagonal, diagonal))
        + np.kron(diagonal, np.kron(slope_table, diagonal))
        + np.kron(diagonal, np.kron(diagonal, slope_table))
    )
    mass_table = np.kron(weights, np.kron(weights, weights))
    face_diag = np.zeros(27)
    select = np.zeros((FACE_ROWS, 2 * ROWS))
    scatter = np.zeros((2 * ROWS, FACE_ROWS))
    for direction in range(3):
        for side in range(2):
            surface = 2 * direction + side
            for major in range(3):
                for minor in range(3):
                    near = [major, minor]
                    near.insert(direction, 2 * side)
                    far = [major, minor]
                    far.insert(direction, 2 - 2 * side)
                    near_node = near[0] * 9 + near[1] * 3 + near[2]
                    far_node = far[0] * 9 + far[1] * 3 + far[2]
                    weight = weights[major] * weights[minor]
                    face_diag[near_node] += weight
                    for part in range(2):
                        row = surface * 18 + part * 9 + major * 3 + minor
                        select[row, part * ROWS + far_node] = -6.0 * penalty * weight
                        scatter[part * ROWS + near_node, row] = 1.0
    block = stiffness + 6.0 * penalty * np.diag(face_diag)
    local = np.zeros((2 * ROWS, 2 * ROWS))
    local[:27, :27] = block
    local[ROWS : ROWS + 27, ROWS : ROWS + 27] = block
    first = np.concatenate([local, select], 0)
    first = np.concatenate([first, first], 1)
    second = np.concatenate([scatter, scatter], 1)
    inverse = np.zeros((ROWS, LANES))
    inverse[:27] = 1.0 / mass_table[:, None]
    return first, second, inverse


def split(values):
    high = values.astype(BF16)
    low = (values - high.astype(F32)).astype(BF16)
    return jnp.concatenate([high, low], 0)


def kernel(
    n_seg, n_sub, old_cuts, new_cuts, start, right, prev, refined, links, first, second, inverse,
    out, state_buf, side_buf, prior_buf, flags, link_buf, first_buf, second_buf, inverse_buf,
    index_buf, block_buf, head_out0, tail_out0, head_in0, tail_in0,
    head_out1, tail_out1, head_in1, tail_in1, ghost_out, ghost_in,
    corner_out, corner_in, moved_buf, load_sem, head_sem, tail_sem, ghost_send, ghost_recv,
    corner_send, corner_recv,
):
    seg, sub = lax.axis_index("seg"), lax.axis_index("sub")
    capacity = links.shape[1]
    blocks = capacity // LANES

    loads = [
        pltpu.make_async_copy(source, target, load_sem.at[i])
        for i, (source, target) in enumerate(
            [
                (start, state_buf),
                (right, side_buf),
                (prev, prior_buf),
                (refined, flags),
                (links, link_buf),
                (first, first_buf),
                (second, second_buf),
                (inverse, inverse_buf),
            ]
        )
    ]
    loads[0].start()

    for arriving in (head_in0, tail_in0, head_in1, tail_in1):
        arriving[...] = jnp.zeros_like(arriving)
    ghost_in[...] = jnp.zeros_like(ghost_in)
    corner_in[...] = jnp.zeros_like(corner_in)

    left = (sub > 0, (seg, sub - 1))
    after = (sub < n_sub - 1, (seg, sub + 1))
    below = (seg > 0, (seg - 1, sub))
    above = (seg < n_seg - 1, (seg + 1, sub))
    above_after = (above[0] & after[0], (seg + 1, sub + 1))
    below_after = (below[0] & after[0], (seg - 1, sub + 1))
    above_left = (above[0] & left[0], (seg + 1, sub - 1))
    below_left = (below[0] & left[0], (seg - 1, sub - 1))
    sides = (left, after, below, above, above_left, below_left)
    barrier = pltpu.get_barrier_semaphore()
    for there, place in sides:
        @pl.when(there)
        def _(place=place):
            pl.semaphore_signal(barrier, inc=1, device_id=place, device_id_type=MESH)
    for load in loads[1:]:
        load.start()

    head_copies = [
        pltpu.make_async_remote_copy(
            src_ref=source, dst_ref=target, send_sem=head_sem.at[i, 0], recv_sem=head_sem.at[i, 1],
            device_id=left[1], device_id_type=MESH)
        for i, (source, target) in enumerate([(head_out0, head_in0), (head_out1, head_in1)])
    ]
    tail_copies = [
        pltpu.make_async_remote_copy(
            src_ref=source, dst_ref=target, send_sem=tail_sem.at[i, 0], recv_sem=tail_sem.at[i, 1],
            device_id=after[1], device_id_type=MESH)
        for i, (source, target) in enumerate([(tail_out0, tail_in0), (tail_out1, tail_in1)])
    ]
    up_copies, down_copies = [], []
    for sweep in range(SWEEPS):
        up_copies.append(pltpu.make_async_remote_copy(
            src_ref=ghost_out.at[sweep], dst_ref=ghost_in.at[sweep, 0],
            send_sem=ghost_send.at[sweep, 0], recv_sem=ghost_recv.at[sweep, 0],
            device_id=above[1], device_id_type=MESH))
        down_copies.append(pltpu.make_async_remote_copy(
            src_ref=ghost_out.at[sweep], dst_ref=ghost_in.at[sweep, 1],
            send_sem=ghost_send.at[sweep, 1], recv_sem=ghost_recv.at[sweep, 1],
            device_id=below[1], device_id_type=MESH))

    corner_up = pltpu.make_async_remote_copy(
        src_ref=corner_out, dst_ref=corner_in.at[0], send_sem=corner_send.at[0],
        recv_sem=corner_recv.at[0], device_id=above_after[1], device_id_type=MESH)
    corner_down = pltpu.make_async_remote_copy(
        src_ref=corner_out, dst_ref=corner_in.at[1], send_sem=corner_send.at[1],
        recv_sem=corner_recv.at[1], device_id=below_after[1], device_id_type=MESH)

    old_first, old_end = old_cuts[0, sub], old_cuts[0, sub + 1]
    new_first, new_end = new_cuts[0, sub], new_cuts[0, sub + 1]
    left_first = old_cuts[0, jnp.maximum(sub - 1, 0)]
    old_count, new_count = old_end - old_first, new_end - new_first
    shift = new_first - old_first
    mask = LANES - 1
    lane = lax.broadcasted_iota(jnp.int32, (8, LANES), 1)
    row = lax.broadcasted_iota(jnp.int32, (8, LANES), 0)

    def wide(values, rows):
        return jnp.broadcast_to(values[:1], (rows, LANES))

    def lanes(rows):
        return lax.broadcasted_iota(jnp.int32, (rows, LANES), 1)

    pad = jnp.zeros((ROWS - 27, LANES), F32)
    row32 = lax.broadcasted_iota(jnp.int32, (ROWS, LANES), 0)

    def component(buffer, b, part):
        rows = buffer[pl.ds(2 * b + part, 27, stride=2 * blocks), :]
        return jnp.concatenate([rows, pad], 0)

    def pack_edges(whole, head_out, tail_out):
        count = whole[0].shape[0]
        upper = count // 2
        lane_u, lane_a = lanes(upper), lanes(count)
        head_out[...] = jnp.where(
            lane_u < HALF, whole[0][:upper], pltpu.roll(whole[0][upper:], HALF, 1)
        )
        tail = whole[0]
        window = (lane_u >= old_count - HALF) & (lane_u < old_count)
        for b in range(1, blocks):
            slot = lane_a + b * LANES
            inside = (slot >= old_count - HALF) & (slot < old_count)
            tail = jnp.where(inside, whole[b], tail)
            slot_u = lane_u + b * LANES
            window = window | ((slot_u >= old_count - HALF) & (slot_u < old_count))
        tail_out[...] = jnp.where(window, tail[:upper], pltpu.roll(tail[upper:], HALF, 1))
        return tail

    def start_edges(i):
        @pl.when(after[0])
        def _():
            tail_copies[i].start()

        @pl.when(left[0])
        def _():
            head_copies[i].start()

    def rotate(whole, first_row):
        turned = [pltpu.roll(w, turn, 1) for w in whole]
        came_from = lanes(whole[0].shape[0]) + shift
        for b in range(blocks):
            mine = turned[b]
            if b > 0:
                mine = jnp.where(came_from < 0, turned[b - 1], mine)
            if b < blocks - 1:
                mine = jnp.where(came_from >= LANES, turned[b + 1], mine)
            rows = slice(first_row, first_row + whole[0].shape[0])
            moved_buf[rows, b * LANES : (b + 1) * LANES] = mine

    def from_edge(arrived, amount):
        return jnp.concatenate(
            [
                pltpu.roll(arrived[...], amount & mask, 1),
                pltpu.roll(arrived[...], (amount + HALF) & mask, 1),
            ],
            0,
        )

    edge = old_end - new_first

    def arrive(i, first_row, count, head_in, tail_in):
        @pl.when(left[0])
        def _():
            tail_copies[i].wait_recv()

        @pl.when(after[0])
        def _():
            head_copies[i].wait_recv()

        from_left = from_edge(tail_in, left_first - new_first)
        from_right = from_edge(head_in, edge)
        lane_a = lanes(count)
        result = []
        for b in range(blocks):
            slot = lane_a + b * LANES
            part = moved_buf[first_row : first_row + count, b * LANES : (b + 1) * LANES]
            if b == 0:
                part = jnp.where(slot < -shift, from_left, part)
            part = jnp.where(slot >= edge, from_right, part)
            result.append(jnp.where(slot < new_count, part, 0.0))
        return result

    loads[0].wait()
    whole = [
        jnp.concatenate([component(state_buf, b, 0), component(state_buf, b, 1)], 0)
        for b in range(blocks)
    ]
    turn = (-shift) & mask
    lane32 = lanes(ROWS)
    slot32 = lane32 & (HALF - 1)

    def both(rows, amount):
        return jnp.where(
            lane32 < HALF,
            pltpu.roll(rows[:ROWS], amount & mask, 1),
            pltpu.roll(rows[ROWS : 2 * ROWS], (amount + HALF) & mask, 1),
        )

    ghost_out[0] = jnp.where(
        (slot32 >= -shift) & (slot32 < new_count), both(whole[0], turn), 0.0
    )
    loads[4].wait()
    for b in range(blocks):
        cols = pl.ds(b * LANES, LANES)
        rows = [jnp.broadcast_to(link_buf[f : f + 1, cols], (8, LANES)) for f in range(6)]
        parts = []
        for k in range(FACE_ROWS // 8):
            f0, f1 = min(8 * k // 18, 5), min((8 * k + 7) // 18, 5)
            part = rows[f0]
            if f1 != f0:
                part = jnp.where(row < f1 * 18 - 8 * k, part, rows[f1])
            parts.append(part)
        link = jnp.concatenate(parts, 0)
        index_buf[:, cols] = link & mask
        block_buf[:, cols] = link >> 7
    seg_sides = jnp.minimum(seg, 1) + jnp.minimum(n_seg - 1 - seg, 1)
    has_after = jnp.minimum(n_sub - 1 - sub, 1)
    pl.semaphore_wait(barrier, jnp.minimum(sub, 1) + has_after + seg_sides * (1 + has_after))

    for there, copy in ((above[0], up_copies[0]), (below[0], down_copies[0])
    ):
        @pl.when(there)
        def _(copy=copy):
            copy.start()

    tail = pack_edges(whole, head_out0, tail_out0)

    start_edges(0)

    next_count = new_cuts[0, jnp.minimum(sub + 2, n_sub)] - new_end
    corner_out[...] = jnp.where(
        (slot32 < old_end - new_end) & (slot32 < next_count), both(tail, old_first - new_end), 0.0
    )

    for there, copy in ((above_after[0], corner_up), (below_after[0], corner_down)
    ):
        @pl.when(there)
        def _(copy=copy):
            copy.start()

    for i in range(1, 4):
        loads[i].wait()
    others = []
    for b in range(blocks):
        cols = pl.ds(b * LANES, LANES)
        flag = flags[:, cols].astype(F32)
        prior = jnp.concatenate([prior_buf[:, cols], pad], 0)
        prior = jnp.where(row32 == 27, jnp.broadcast_to(flag, (ROWS, LANES)), prior)
        others.append(
            jnp.concatenate([component(side_buf, b, 0), component(side_buf, b, 1), prior], 0)
        )
    pack_edges(others, head_out1, tail_out1)
    start_edges(1)
    rotate(whole, 0)

    for i in range(5, 8):
        loads[i].wait()

    def send(sweep, c, mu):
        ghost_out[sweep] = jnp.where(lane32 < HALF, c, pltpu.roll(mu, HALF, 1))

        @pl.when(above[0])
        def _():
            up_copies[sweep].start()

        @pl.when(below[0])
        def _():
            down_copies[sweep].start()

    state = arrive(0, 0, 2 * ROWS, head_in0, tail_in0)
    rotate(others, 2 * ROWS)

    def coefficients_of():
        result = []
        inverse_mass = inverse_buf[...]
        for part in arrive(1, 2 * ROWS, 3 * ROWS, head_in1, tail_in1):
            prior = part[2 * ROWS :]
            flag = jnp.broadcast_to(prior[27:28], (ROWS, LANES))
            inverse_lumped = inverse_mass * (1.0 + 7.0 * flag)
            stiff = (1.0 - 0.5 * flag) * inverse_lumped * (1.0 / 6.0)
            result.append(
                (
                    part[:ROWS] * inverse_lumped,
                    part[ROWS : 2 * ROWS] * inverse_lumped,
                    time_step * stiff * (1.0 - prior * prior),
                    gradient_energy * stiff,
                    3.0 * prior * prior - 1.0,
                )
            )
        return result

    spread_ratio = 2.0
    half_width = 0.5
    weight_prev = 1.0 / spread_ratio
    update = [None] * blocks
    first_table, second_table = first_buf[...], second_buf[...]
    for sweep in range(SWEEPS):
        last = sweep == SWEEPS - 1
        product = jnp.dot(
            first_table, jnp.concatenate([split(v) for v in state], 1), preferred_element_type=F32
        )
        near = product[: 2 * ROWS]
        sources = [product[2 * ROWS :, b * LANES : (b + 1) * LANES] for b in range(blocks)]

        def pick(total, source, number, b):
            cols = slice(b * LANES, (b + 1) * LANES)
            index = index_buf[:, cols]
            got = jnp.take_along_axis(source, index, axis=1, mode="promise_in_bounds")
            return jnp.where(block_buf[:, cols] == number, got, total)

        faces = []
        for b in range(blocks):
            total = jnp.zeros((FACE_ROWS, LANES), F32)
            for number in range(blocks):
                total = pick(total, sources[number], number, b)
            faces.append(total)
        if sweep == 0:
            coefficients = coefficients_of()

        @pl.when(below[0])
        def _():
            up_copies[sweep].wait_recv()

        @pl.when(above[0])
        def _():
            down_copies[sweep].wait_recv()

        got_below, got_above = ghost_in[sweep, 0], ghost_in[sweep, 1]
        if sweep == 0:
            @pl.when(below_left[0])
            def _():
                corner_up.wait_recv()

            @pl.when(above_left[0])
            def _():
                corner_down.wait_recv()

            got_below = got_below + corner_in[0]
            got_above = got_above + corner_in[1]
        ghost = jnp.concatenate(
            [
                jnp.where(lane32 < HALF, got_below, pltpu.roll(got_above, HALF, 1)),
                jnp.where(lane32 < HALF, pltpu.roll(got_below, HALF, 1), got_above),
            ],
            0,
        )
        ghost_faces = jnp.dot(first_table[2 * ROWS :], split(ghost), preferred_element_type=F32)

        weight_now = 1.0 / (2.0 * spread_ratio - weight_prev)
        for b in range(blocks):
            total = pick(faces[b], ghost_faces, blocks, b)
            coupled = jnp.dot(second_table, split(total), preferred_element_type=F32)
            laplace = near[:, b * LANES : (b + 1) * LANES] + coupled
            side_c, side_mu, mobile, stiff, curvature = coefficients[b]
            c, mu = state[b][:ROWS], state[b][ROWS:]
            scaled = jnp.concatenate(
                [
                    side_c - c - mobile * laplace[ROWS:],
                    side_mu - mu + curvature * c + stiff * laplace[:ROWS],
                ],
                0,
            )
            if sweep == 0:
                update[b] = scaled
            else:
                update[b] = (
                    weight_now * weight_prev * update[b] + (2.0 * weight_now / half_width) * scaled
                )
            state[b] = state[b] + update[b]
            if last:
                out[pl.ds(2 * b, 27, stride=2 * blocks), :] = state[b][:27]
                out[pl.ds(2 * b + 1, 27, stride=2 * blocks), :] = state[b][ROWS : ROWS + 27]
            elif b == 0:
                send(sweep + 1, state[0][:ROWS], state[0][ROWS:])
        if sweep > 0:
            weight_prev = weight_now

    @pl.when(left[0])
    def _():
        for copy in head_copies:
            copy.wait_send()

    @pl.when(after[0])
    def _():
        for copy in tail_copies:
            copy.wait_send()

    @pl.when(above_after[0])
    def _():
        corner_up.wait_send()

    @pl.when(below_after[0])
    def _():
        corner_down.wait_send()

    for sweep in range(SWEEPS):
        @pl.when(above[0])
        def _():
            up_copies[sweep].wait_send()

        @pl.when(below[0])
        def _():
            down_copies[sweep].wait_send()


def local(n_seg, n_sub, start_state, right_side, previous, refined, old_cuts, new_cuts, face_links):
    capacity = start_state.shape[-1]
    first, second, inverse = element_tables()
    any_space = pl.BlockSpec(memory_space=pl.ANY)
    smem = pl.BlockSpec(memory_space=pltpu.SMEM)
    blocks = capacity // LANES

    def by_node(array):
        array = array.transpose(1, 0, 2).reshape(27, 2, blocks, LANES)
        return array.transpose(0, 2, 1, 3).reshape(54 * blocks, LANES)

    smoothed = pl.pallas_call(
        functools.partial(kernel, n_seg, n_sub),
        out_shape=pltpu.VMEM((54 * blocks, LANES), F32),
        in_specs=[smem, smem] + [any_space] * 8,
        out_specs=pl.BlockSpec(memory_space=pltpu.VMEM),
        scratch_shapes=[
            pltpu.VMEM((54 * blocks, LANES), F32),
            pltpu.VMEM((54 * blocks, LANES), F32),
            pltpu.VMEM((27, capacity), F32),
            pltpu.VMEM((1, capacity), jnp.int32),
            pltpu.VMEM((6, capacity), jnp.int32),
            pltpu.VMEM(first.shape, BF16),
            pltpu.VMEM(second.shape, BF16),
            pltpu.VMEM(inverse.shape, F32),
            pltpu.VMEM((FACE_ROWS, capacity), jnp.int32),
            pltpu.VMEM((FACE_ROWS, capacity), jnp.int32),
            *[pltpu.VMEM((ROWS, LANES), F32)] * 4,
            *[pltpu.VMEM((3 * ROWS // 2, LANES), F32)] * 4,
            pltpu.VMEM((SWEEPS, ROWS, LANES), F32),
            pltpu.VMEM((SWEEPS, 2, ROWS, LANES), F32),
            pltpu.VMEM((ROWS, LANES), F32),
            pltpu.VMEM((2, ROWS, LANES), F32),
            pltpu.VMEM((5 * ROWS, capacity), F32),
            pltpu.SemaphoreType.DMA((8,)),
            pltpu.SemaphoreType.DMA((2, 2)),
            pltpu.SemaphoreType.DMA((2, 2)),
            pltpu.SemaphoreType.DMA((SWEEPS, 2)),
            pltpu.SemaphoreType.DMA((SWEEPS, 2)),
            pltpu.SemaphoreType.DMA((2,)),
            pltpu.SemaphoreType.DMA((2,)),
        ],
        compiler_params=pltpu.CompilerParams(
            collective_id=0, has_side_effects=True, vmem_limit_bytes=60 * 1024 * 1024
        ),
        name="smooth",
    )(
        old_cuts, new_cuts, by_node(start_state), by_node(right_side), previous,
        refined.reshape(1, capacity),
        face_links, jnp.asarray(first, BF16), jnp.asarray(second, BF16), jnp.asarray(inverse, F32),
    )
    smoothed = smoothed.reshape(27, blocks, 2, LANES).transpose(2, 0, 1, 3)
    return smoothed.reshape(2, 27, capacity)


def solution(mesh):
    placed = (
        P(None, None, ("seg", "sub")),
        P(None, None, ("seg", "sub")),
        P(None, ("seg", "sub")),
        P(("seg", "sub")),
        P("seg", None),
        P("seg", None),
        P(None, ("seg", "sub")),
    )
    return jax.shard_map(
        functools.partial(local, mesh.shape["seg"], mesh.shape["sub"]),
        mesh=mesh, in_specs=placed, out_specs=P(None, None, ("seg", "sub")), check_vma=False,
    )
```
